32 devices in a mesh: group: 2 (over y), pool: 2 (over core), dev: 8 (over z, x).
Axes of the slice: x: 2, y: 2, z: 4, core: 2. Of those that a mesh axis runs over, the one named last changes fastest.
Arguments:
- tokens: bfloat16 [2, 1024, 7168], P(None, ('group', 'pool', 'dev')), parts along dimension 1, may hold values from -6 to 6
- routes: int32 [2, 1024, 8], P(None, ('group', 'pool', 'dev')), parts along dimension 1, may hold values from 0 to 255, all different within a row; in each aligned block of 32 rows (0 to 31, 32 to 63, ..., all dimensions but the last counted through in order) at most 2 rows name the same one
- router: bfloat16 [256, 7168], P(('pool', 'dev')), may hold values from -0.0625 to 0.0625
- w_gate: bfloat16 [7168, 4096], P(None, ('pool', 'dev')), may hold values from -0.0625 to 0.0625
- w_up: bfloat16 [7168, 4096], P(None, ('pool', 'dev')), may hold values from -0.0625 to 0.0625
- w_down: bfloat16 [4096, 7168], P(('pool', 'dev')), may hold values from -0.125 to 0.125
Outputs:
- combined: bfloat16 [2, 1024, 7168], P(None, ('group', 'pool', 'dev')), parts along dimension 1
The draws below stay inside these ranges and needn't reach their ends.
There are 2 independent parts, one for each index of `group`. The reference program is written for one: setup_inputs(seed, part) draws one part's arguments, and reference() takes and returns one part's arrays. A program takes and returns all parts, laid end to end along the dimension named above; an argument that names none is the same for every part. Nothing has to cross between parts.
Inputs may be any that keep to these rules, and one draw needn't show every extreme that they name: `routes`: each row names 8 different experts; in each micro-batch the rows of one device name no expert more than 2 times, a bound that some block reaches.
All inputs are finite; a program needn't handle non-finite values.
Results may differ from the reference program's by a relative error of at most 0.009.
Values may be sent and summed in bfloat16 or wider, within the bound.
A program may use at most 128 MiB of HBM per device.

```python
import math
import jax
import jax.numpy as jnp
import numpy as np
from jax import lax

D = 7168
FF = 2048
EXPERTS = 256
TOP = 8
HID_DEV = 256
MB = 2
ROWS_MB = 32
CAP = 2
SLICES = 8
EXP_WIN = 2
ROWS = 512


def block_levels(rng, shape, cuts, low, largest):
    def one(dim, parts):
        heights = jax.random.uniform(jax.random.fold_in(jax.random.fold_in(rng, 6), dim), (parts,), jnp.float32, low / len(cuts), largest / len(cuts))
        return jnp.repeat(jnp.exp(heights), shape[dim] // parts).reshape((-1,) + (1,) * (len(shape) - dim - 1))

    factor_of = one(*cuts[0])
    for cut in cuts[1:]:
        factor_of = factor_of * one(*cut)
    return factor_of


def assign_block(key, own, number, rows, amount, top, most, skew):
    ranking = jax.random.permutation(key, amount)
    heavy_load, usual = shares(amount, rows * top, most, skew, True), shares(amount, rows * top, most, skew, False)
    places = jnp.arange(amount)

    def named(sizes, offset_by):
        used = int((sizes > 0).sum())
        fixed = max(1, used // 4)
        moved = fixed + (places - fixed + offset_by * (used - fixed)) % max(1, amount - fixed)
        return jnp.zeros((amount,), jnp.int32).at[ranking[jnp.where(places < fixed, places, moved)]].set(jnp.asarray(sizes, jnp.int32))

    sizes = jnp.where(number % 4 == 0, named(heavy_load, number // 4), named(usual, number - number // 4 - 1))
    mixed = jax.random.permutation(jax.random.fold_in(own, 3), amount)
    donor, sink = mixed[0:amount // 2 * 2:2], mixed[1:amount // 2 * 2:2]
    room = jnp.minimum(sizes[donor] - 1, most - sizes[sink]) // 2
    room = jnp.where((donor == ranking[0]) | (sink == ranking[0]) | (sizes[sink] == 0), 0, jnp.maximum(room, 0))
    moved = jax.random.randint(jax.random.fold_in(own, 4), (amount // 2,), 0, 1 << 20) % (room + 1)
    sizes = sizes.at[donor].add(-moved).at[sink].add(moved)
    labels = jnp.searchsorted(jnp.cumsum(sizes), jnp.arange(rows * top), side="right").astype(jnp.int32)
    grid = labels.reshape(top, rows).T
    grid = grid[jax.random.permutation(jax.random.fold_in(own, 1), rows)]
    offset_by = jax.random.randint(jax.random.fold_in(own, 2), (rows, 1), 0, top)
    return jnp.take_along_axis(grid, (jnp.arange(top)[None, :] + offset_by) % top, axis=1)


def shares(count, total, bound, skew, full):
    portions = [(1 << 20) // math.isqrt(standing ** skew) + 1 for standing in range(1, count + 1)]
    largest = bound if full else min(bound, max(-(-total // count), total * portions[0] // sum(portions)))
    least = 1 if total - largest >= count - 1 else 0
    holding, spare = [largest] + [least] * (count - 1), total - largest - least * (count - 1)
    while spare > 0:
        candidates = [i for i in range(1, count) if holding[i] < largest] or [i for i in range(1, count) if holding[i] < bound]
        pool, budget = sum([portions[i] for i in candidates]), spare
        for i in candidates:
            addition = min(bound - holding[i], max(1, budget * portions[i] // pool), spare)
            holding[i] = holding[i] + addition
            spare = spare - addition
    return np.array(holding)


def normal_values(key, extent, deviation, reach, shards=(), held_as=jnp.bfloat16):
    level = block_levels(key, extent, shards, -0.22, 0.18) if shards else 1.0
    drawn = jax.random.normal(key, extent, jnp.float32) * deviation * level
    return jnp.minimum(jnp.maximum(drawn, -reach), reach).astype(held_as)


def setup_inputs(seed: int = 0, part: int = 0) -> dict:
    streams_of = jax.random.split(jax.random.key(seed), 7)
    part_splits = jax.random.split(jax.random.fold_in(streams_of[6], part), 7)
    tokens = normal_values(part_splits[0], (MB, ROWS, D), 1.0, 6.0, ((1, 16),))
    routes_keys = jax.random.split(jax.random.fold_in(part_splits[1], 1), MB * ROWS // ROWS_MB)
    routes_turns = jax.random.permutation(jax.random.fold_in(part_splits[1], 3), MB * ROWS // ROWS_MB)
    routes = jax.vmap(lambda own, number: assign_block(jax.random.fold_in(part_splits[1], 2), own, number, ROWS_MB, EXPERTS, TOP, CAP, 2))(routes_keys, routes_turns).reshape((MB, ROWS, TOP))
    router = normal_values(streams_of[2], (EXPERTS, D), D ** -0.5, 0.0625, ((0, 16),))
    w_gate = normal_values(streams_of[3], (D, EXP_WIN * FF), D ** -0.5, 0.0625, ((1, 16),))
    w_up = normal_values(streams_of[4], (D, EXP_WIN * FF), D ** -0.5, 0.0625, ((1, 16),))
    w_down = normal_values(streams_of[5], (EXP_WIN * FF, D), FF ** -0.5, 0.125, ((0, 16),))
    return dict(tokens=tokens, routes=routes, router=router, w_gate=w_gate, w_up=w_up, w_down=w_down)


route_scale = 2.5


def reference(tokens, routes, router, w_gate, w_up, w_down):
    batches = tokens.shape[0]
    total_rows = tokens.shape[1]
    model_width = tokens.shape[2]
    blocks = total_rows // ROWS_MB
    logits = jnp.einsum("mrd,ed->mre", tokens.astype(jnp.float32), router.astype(jnp.float32))
    scores = jax.nn.sigmoid(logits)
    expert_ids = jnp.arange(EXPERTS, dtype=jnp.int32)
    picked = routes[..., None] == expert_ids
    chosen = jnp.sum(jnp.where(picked, scores[:, :, None, :], 0.0), axis=-1)
    weights = route_scale * chosen / jnp.sum(chosen, axis=-1, keepdims=True)
    window = picked[..., :EXP_WIN]
    route_weight = jnp.sum(jnp.where(window, weights[..., None], 0.0), axis=2)
    routed = jnp.any(window, axis=2).astype(jnp.int32)
    routed = routed.reshape(batches, blocks, ROWS_MB, EXP_WIN)
    route_weight = route_weight.reshape(batches, blocks, ROWS_MB, EXP_WIN)
    position = jnp.cumsum(routed, axis=2) - 1
    slot_ids = jnp.arange(CAP, dtype=jnp.int32)
    selector = ((routed[..., None] == 1) & (position[..., None] == slot_ids)).astype(jnp.float32)
    blocked = tokens.reshape(batches, blocks, ROWS_MB, model_width).astype(jnp.float32)

    def add_expert(expert, summed):
        sel_one = lax.dynamic_index_in_dim(selector, expert, 3, keepdims=False)
        weight_one = lax.dynamic_index_in_dim(route_weight, expert, 3, keepdims=False)
        gathered = jnp.einsum("mbrc,mbrd->mbcd", sel_one, blocked).astype(jnp.bfloat16)
        flat_rows = gathered.reshape(-1, model_width)
        gate_cols = lax.dynamic_slice_in_dim(w_gate, expert * FF, FF, 1)
        up_cols = lax.dynamic_slice_in_dim(w_up, expert * FF, FF, 1)
        gate_proj = jnp.dot(flat_rows, gate_cols, preferred_element_type=jnp.float32)
        up_proj = jnp.dot(flat_rows, up_cols, preferred_element_type=jnp.float32)
        hidden = (jax.nn.silu(gate_proj) * up_proj).astype(jnp.bfloat16)
        down_rows = lax.dynamic_slice_in_dim(w_down, expert * FF, FF, 0)
        down_rows = down_rows.reshape(SLICES, HID_DEV, model_width).astype(jnp.float32)
        hidden_split = hidden.reshape(-1, SLICES, HID_DEV).astype(jnp.float32)
        partial_value = jnp.einsum("nsh,shd->nsd", hidden_split, down_rows).astype(jnp.bfloat16)
        expert_out = jnp.sum(partial_value.astype(jnp.float32), axis=1)
        expert_out = expert_out.reshape(batches, blocks, CAP, model_width)
        mixing = sel_one * weight_one[..., None]
        return summed + jnp.einsum("mbrc,mbcd->mbrd", mixing, expert_out, precision=lax.Precision.HIGHEST)

    start_sum = jnp.zeros((batches, blocks, ROWS_MB, model_width), jnp.float32)
    summed = lax.fori_loop(0, EXP_WIN, add_expert, start_sum)
    return summed.reshape(batches, total_rows, model_width).astype(jnp.bfloat16)
```

```python
import functools

import jax
import jax.numpy as jnp
from jax import lax
from jax.experimental import pallas as pl
from jax.experimental.pallas import tpu as pltpu
from jax.sharding import PartitionSpec as P

FF = 2048
CAP = 2
LINE = 4
PAIR = 2

route_scale = 2.5
MESH = pl.DeviceIdType.MESH
F32 = jnp.float32
BF16 = jnp.bfloat16


def dot(a, b):
    return jnp.dot(a, b, preferred_element_type=F32)


def dot_tn(a, b):
    return lax.dot_general(a, b, (((0,), (0,)), ((), ())), preferred_element_type=F32)


def dot_nt(a, b):
    return lax.dot_general(a, b, (((1,), (1,)), ((), ())), preferred_element_type=F32)


def kernel(
    tokens, routes, router, w_gate, w_up, w_down, out,
    gate_v, up_v, down_v, router_v, mine, theirs, rows, parts, from_x, from_up, from_down, sums,
    total_v, total_peer, logit_out, logit_in, logit_peer,
    load_sem, peer_send, peer_recv, row_recv, row_up, row_down, row_x,
    log_send, log_recv, x_send, x_recv, up_send, up_recv, down_send, down_recv,
):
    pool, dev = lax.axis_index("pool"), lax.axis_index("dev")
    chips = LINE * PAIR
    line, pair = dev // PAIR, dev % PAIR
    n_rows, width = tokens.shape
    half = width // 2
    block = n_rows // 2
    router_rows = router.shape[0]

    loads = [
        pltpu.make_async_copy(w_gate, gate_v, load_sem.at[0]),
        pltpu.make_async_copy(w_up, up_v, load_sem.at[1]),
        pltpu.make_async_copy(w_down, down_v, load_sem.at[2]),
    ]
    for load in loads:
        load.start()

    barrier = pltpu.get_barrier_semaphore()
    pl.semaphore_signal(barrier, inc=1, device_id={"pool": 1 - pool}, device_id_type=MESH)
    for step in range(1, chips):
        pl.semaphore_signal(
            barrier, inc=1, device_id={"dev": lax.rem(dev + step, chips)}, device_id_type=MESH
        )

    ids = routes[...]
    row_no = lax.broadcasted_iota(jnp.int32, (n_rows, 8), 0)
    slot_no = lax.broadcasted_iota(jnp.int32, (n_rows, 8), 1)
    place = (row_no // block == (slot_no % 4) // 2) & (slot_no // 4 == pool)
    r0 = lax.broadcasted_iota(jnp.int32, (n_rows, n_rows), 0)
    r1 = lax.broadcasted_iota(jnp.int32, (n_rows, n_rows), 1)
    earlier = ((r1 < r0) & (r0 // block == r1 // block)).astype(F32).astype(BF16)

    def select(expert):
        named = jnp.max((ids == expert).astype(F32), axis=1, keepdims=True)
        named = jnp.broadcast_to(named, (n_rows, 8))
        count = dot(earlier, named.astype(BF16))
        hit = (named > 0.5) & place & (count == (slot_no % 2).astype(F32))
        return hit.astype(F32)

    def in_slots(sel):
        sel = sel.astype(BF16)
        left = dot_tn(sel, tokens[:, :half])
        right = dot_tn(sel, tokens[:, half:])
        return jnp.concatenate([left, right], axis=0).astype(BF16)

    sel_own, sel_other = select(pool), select(1 - pool)
    mine[...] = in_slots(sel_other)
    router_v[pool] = router[...]

    pl.semaphore_wait(barrier, chips)

    def to_peer(src, dst, k):
        return pltpu.make_async_remote_copy(
            src, dst, peer_send.at[k], peer_recv.at[k],
            device_id={"pool": 1 - pool}, device_id_type=MESH,
        )

    peer_rows = to_peer(mine, theirs, 0)
    peer_rows.start()
    peer_router = to_peer(router_v.at[pool], router_v.at[pool], 1)
    peer_router.start()
    own = in_slots(sel_own)
    peer_rows.wait_recv()
    rows[dev] = own + theirs[...]

    def row_copy(z, target, sems):
        c = z * PAIR + pair
        return pltpu.make_async_remote_copy(
            rows.at[c], rows.at[c], sems.at[z], row_recv.at[c],
            device_id={"dev": target}, device_id_type=MESH,
        )

    def row_wait(c):
        pltpu.make_async_copy(rows.at[c], rows.at[c], row_recv.at[c]).wait()

    across = line * PAIR + 1 - pair

    @pl.when(line < LINE - 1)
    def _():
        row_copy(line, dev + PAIR, row_up).start()

    @pl.when(line > 0)
    def _():
        row_copy(line, dev - PAIR, row_down).start()

    row_copy(line, across, row_x).start()
    for d in range(1, LINE):
        @pl.when(line - d >= 0)
        def _():
            z = line - d
            row_wait(z * PAIR + pair)

            @pl.when(line < LINE - 1)
            def _():
                row_copy(z, dev + PAIR, row_up).start()

            row_copy(z, across, row_x).start()

        @pl.when(line + d < LINE)
        def _():
            z = line + d
            row_wait(z * PAIR + pair)

            @pl.when(line > 0)
            def _():
                row_copy(z, dev - PAIR, row_down).start()

            row_copy(z, across, row_x).start()

    for z in range(LINE):
        row_wait(z * PAIR + 1 - pair)
    peer_router.wait_recv()
    for load in loads:
        load.wait()

    tile = half // 4
    hid = gate_v.shape[1]

    def project(side):
        def body(k, carry):
            g, u, l = carry
            at = pl.multiple_of(k * tile, 128)
            deep = pl.multiple_of(side * half + k * tile, 128)
            a = rows[:, :, pl.ds(at, tile)].reshape(chips * 16, tile)
            r = router_v[:, :, pl.ds(deep, tile)].reshape(2 * router_rows, tile)
            g = g + dot(a, gate_v[pl.ds(deep, tile), :])
            u = u + dot(a, up_v[pl.ds(deep, tile), :])
            l = l + dot_nt(a, r)
            return g, u, l

        zero = jnp.zeros((chips * 16, hid), F32)
        got = lax.fori_loop(
            0, 4, body, (zero, zero, jnp.zeros((chips * 16, 2 * router_rows), F32))
        )
        return [v.reshape(chips, 16, v.shape[1])[:, side * 8 : side * 8 + 8] for v in got]

    (gl, ul, ll), (gr, ur, lr) = project(0), project(1)
    gate, up = gl + gr, ul + ur
    hidden = (gate / (1.0 + jnp.exp(-gate)) * up).astype(F32).reshape(chips * 8, hid).astype(BF16)
    logit_out[:, :, 0 : 2 * router_rows] = ll + lr
    logit_out[:, :, 2 * router_rows :] = jnp.zeros((chips, 8, 128 - 2 * router_rows), F32)
    logit_in[dev] = logit_out[dev]

    def log_copy(step):
        to = lax.rem(dev + step, chips)
        return pltpu.make_async_remote_copy(
            logit_out.at[to], logit_in.at[dev], log_send.at[step], log_recv.at[dev],
            device_id={"dev": to}, device_id_type=MESH,
        )

    for step in range(1, chips):
        log_copy(step).start()

    def down(t, _):
        at = pl.multiple_of(t * tile, 128)
        left = dot(hidden, down_v[:, pl.ds(at, tile)]).reshape(chips, 8, tile)
        right = dot(hidden, down_v[:, pl.ds(pl.multiple_of(half + at, 128), tile)]).reshape(chips, 8, tile)
        parts[:, :, pl.ds(at, tile)] = jnp.concatenate([left, right], axis=1).astype(BF16)
        return 0

    lax.fori_loop(0, 4, down, 0)

    def x_copy(z):
        return pltpu.make_async_remote_copy(
            parts.at[z * PAIR + 1 - pair], from_x.at[z], x_send.at[z], x_recv.at[z],
            device_id={"dev": across}, device_id_type=MESH,
        )

    def up_copy(z):
        return pltpu.make_async_remote_copy(
            sums.at[z], from_up.at[z], up_send.at[z], up_recv.at[z],
            device_id={"dev": dev + PAIR}, device_id_type=MESH,
        )

    def down_copy(z):
        return pltpu.make_async_remote_copy(
            sums.at[z], from_down.at[z], down_send.at[z], down_recv.at[z],
            device_id={"dev": dev - PAIR}, device_id_type=MESH,
        )

    def each_far_first(act_up, act_down):
        for d in range(LINE - 1, 0, -1):
            @pl.when(line + d < LINE)
            def _():
                act_up(line + d)

            @pl.when(line - d >= 0)
            def _():
                act_down(line - d)

    each_far_first(lambda z: x_copy(z).start(), lambda z: x_copy(z).start())
    x_copy(line).start()

    def paired(z):
        x_copy(z).wait_recv()
        return parts[z * PAIR + pair].astype(F32) + from_x[z].astype(F32)

    def go_up(z):
        total = paired(z)
        sums[z] = total.astype(BF16)

        @pl.when(line > 0)
        def _():
            up_copy(z).wait_recv()
            sums[z] = (total + from_up[z].astype(F32)).astype(BF16)

        up_copy(z).start()

    def go_down(z):
        total = paired(z)
        sums[z] = total.astype(BF16)

        @pl.when(line < LINE - 1)
        def _():
            down_copy(z).wait_recv()
            sums[z] = (total + from_down[z].astype(F32)).astype(BF16)

        down_copy(z).start()

    each_far_first(go_up, go_down)
    total_v[...] = paired(line)

    for step in range(1, chips):
        c = lax.rem(dev + step, chips)
        pltpu.make_async_copy(logit_in.at[c], logit_in.at[c], log_recv.at[c]).wait()
    peer_logits = to_peer(logit_in, logit_peer, 2)
    peer_logits.start()

    @pl.when(line > 0)
    def _():
        up_copy(line).wait_recv()
        total_v[...] += from_up[line].astype(F32)

    @pl.when(line < LINE - 1)
    def _():
        down_copy(line).wait_recv()
        total_v[...] += from_down[line].astype(F32)

    peer_total = to_peer(total_v, total_peer, 3)
    peer_total.start()

    lane = lax.broadcasted_iota(jnp.int32, (8, 128), 1)
    id_bf16 = ids.astype(F32).astype(BF16)

    def weigh(sel, logits, expert):
        named = dot_tn(sel.astype(BF16), id_bf16)
        near = jnp.zeros((8, 128), F32)
        every = jnp.zeros((8, 128), F32)
        for s in range(chips):
            number = (lane // router_rows) * (chips * router_rows) + s * router_rows + lane % router_rows
            number = jnp.where(lane < 2 * router_rows, number, -1)
            score = 1.0 / (1.0 + jnp.exp(-logits[s]))
            near += jnp.where(number == expert, score, 0.0)
            match = number.astype(F32) == named[:, 0:1]
            for k in range(1, ids.shape[1]):
                match |= number.astype(F32) == named[:, k : k + 1]
            every += jnp.where(match, score, 0.0)
        near = jnp.sum(near, axis=1, keepdims=True)
        every = jnp.sum(every, axis=1, keepdims=True)
        return route_scale * near / every

    def split(total, weight):
        j = lax.broadcasted_iota(jnp.int32, (8, 1), 0)
        both = []
        for side in range(2):
            v = jnp.where(j // 4 == pool, total[side * 8 : side * 8 + 8] * weight, 0.0)
            hi = v.astype(BF16).astype(F32)
            both.append(jnp.concatenate([hi, v - hi], axis=0).astype(BF16))
        return both

    own_weight = weigh(sel_own, logit_in, pool)
    own_left, own_right = split(total_v[...], own_weight)
    peer_logits.wait_recv()
    other_weight = weigh(sel_other, logit_peer, 1 - pool)
    peer_total.wait_recv()
    other_left, other_right = split(total_peer[...], other_weight)
    so, st = sel_own.astype(BF16), sel_other.astype(BF16)
    mixing = jnp.concatenate([so, so, st, st], axis=1)
    out[:, :half] = dot(mixing, jnp.concatenate([own_left, other_left], axis=0)).astype(BF16)
    out[:, half:] = dot(mixing, jnp.concatenate([own_right, other_right], axis=0)).astype(BF16)

    for copy in (peer_rows, peer_router, peer_logits, peer_total):
        copy.wait_send()
    for z in range(LINE):
        row_copy(z, across, row_x).wait_send()
        x_copy(z).wait_send()

        @pl.when((line < LINE - 1) & (z <= line))
        def _():
            row_copy(z, dev + PAIR, row_up).wait_send()

        @pl.when((line > 0) & (z >= line))
        def _():
            row_copy(z, dev - PAIR, row_down).wait_send()

        @pl.when(z > line)
        def _():
            up_copy(z).wait_send()

        @pl.when(z < line)
        def _():
            down_copy(z).wait_send()

    for step in range(1, chips):
        log_copy(step).wait_send()


def fused(tokens, routes, router, w_gate, w_up, w_down):
    batches, block, width = tokens.shape
    half = width // 2
    chips = LINE * PAIR
    n_rows = batches * block
    vmem = pl.BlockSpec(memory_space=pltpu.VMEM)
    hbm = pl.BlockSpec(memory_space=pl.ANY)
    dma = pltpu.SemaphoreType.DMA
    out = pl.pallas_call(
        kernel,
        out_shape=jax.ShapeDtypeStruct((n_rows, width), BF16),
        in_specs=[vmem, vmem, vmem, hbm, hbm, hbm],
        out_specs=vmem,
        scratch_shapes=[
            pltpu.VMEM(w_gate.shape, BF16),
            pltpu.VMEM(w_up.shape, BF16),
            pltpu.VMEM(w_down.shape, BF16),
            pltpu.VMEM((2, router.shape[0], width), BF16),
            pltpu.VMEM((16, half), BF16),
            pltpu.VMEM((16, half), BF16),
            pltpu.VMEM((chips, 16, half), BF16),
            pltpu.VMEM((chips, 16, half), BF16),
            pltpu.VMEM((LINE, 16, half), BF16),
            pltpu.VMEM((LINE, 16, half), BF16),
            pltpu.VMEM((LINE, 16, half), BF16),
            pltpu.VMEM((LINE, 16, half), BF16),
            pltpu.VMEM((16, half), F32),
            pltpu.VMEM((16, half), F32),
            pltpu.VMEM((chips, 8, 128), F32),
            pltpu.VMEM((chips, 8, 128), F32),
            pltpu.VMEM((chips, 8, 128), F32),
            dma((3,)), dma((4,)), dma((4,)), dma((chips,)), dma((LINE,)), dma((LINE,)), dma((LINE,)),
            dma((chips,)), dma((chips,)), dma((LINE,)), dma((LINE,)), dma((LINE,)), dma((LINE,)),
            dma((LINE,)), dma((LINE,)),
        ],
        compiler_params=pltpu.CompilerParams(
            collective_id=0, has_side_effects=True, vmem_limit_bytes=44 << 20
        ),
    )(tokens.reshape(n_rows, width), routes.reshape(n_rows, -1), router, w_gate, w_up, w_down)
    return out.reshape(tokens.shape)


def spread(tokens, routes, router, w_gate, w_up, w_down):
    groups = lax.axis_size(("pool", "dev"))
    batches = tokens.shape[0]
    model_width = tokens.shape[2]
    hidden_width = w_gate.shape[1]
    slices = FF // hidden_width
    experts_win = groups // slices
    capacity = CAP
    logits = jnp.einsum(
        "mrd,ed->mre",
        tokens,
        lax.all_gather(router, ("pool", "dev"), axis=0, tiled=True),
        preferred_element_type=jnp.float32,
    )
    scores = jax.nn.sigmoid(logits)
    expert_ids = jnp.arange(logits.shape[2], dtype=jnp.int32)
    picked = routes[..., None] == expert_ids
    chosen = jnp.sum(jnp.where(picked, scores[:, :, None, :], 0.0), axis=-1)
    weights = route_scale * chosen / jnp.sum(chosen, axis=-1, keepdims=True)
    window = picked[..., :experts_win]
    route_weight = jnp.sum(jnp.where(window, weights[..., None], 0.0), axis=2)
    routed = jnp.any(window, axis=2).astype(jnp.int32)
    position = jnp.cumsum(routed, axis=1) - 1
    slot_ids = jnp.arange(capacity, dtype=jnp.int32)
    selector = (routed[..., None] == 1) & (position[..., None] == slot_ids)
    slot_rows = jnp.einsum(
        "mrec,mrd->mecd", selector.astype(jnp.bfloat16), tokens, preferred_element_type=jnp.float32
    ).astype(jnp.bfloat16)
    outgoing = jnp.broadcast_to(
        slot_rows[:, :, None], (batches, experts_win, slices, capacity, model_width)
    )
    outgoing = outgoing.reshape(batches, groups, capacity, model_width)
    arrived = lax.all_to_all(outgoing, ("pool", "dev"), split_axis=1, concat_axis=1, tiled=True)
    flat_rows = arrived.reshape(-1, model_width)
    gate_proj = jnp.dot(flat_rows, w_gate, preferred_element_type=jnp.float32)
    up_proj = jnp.dot(flat_rows, w_up, preferred_element_type=jnp.float32)
    hidden = (jax.nn.silu(gate_proj) * up_proj).astype(jnp.bfloat16)
    partial_value = jnp.dot(hidden, w_down, preferred_element_type=jnp.float32).astype(jnp.bfloat16)
    send_partial_value = partial_value.reshape(arrived.shape)
    returned = lax.all_to_all(
        send_partial_value, ("pool", "dev"), split_axis=1, concat_axis=1, tiled=True
    )
    returned = returned.reshape(batches, experts_win, slices, capacity, model_width)
    expert_out = jnp.sum(returned, axis=2, dtype=jnp.float32)
    mixing = selector.astype(jnp.float32) * route_weight[..., None]
    combined = jnp.einsum("mrec,mecd->mrd", mixing, expert_out, precision=lax.Precision.HIGHEST)
    return combined.astype(jnp.bfloat16)


def solution(mesh):
    shape = dict(mesh.shape)
    per_device = fused if (shape["pool"], shape["dev"]) == (2, LINE * PAIR) else spread
    placed = (
        P(None, ("group", "pool", "dev"), None),
        P(None, ("group", "pool", "dev"), None),
        P(("pool", "dev"), None),
        P(None, ("pool", "dev")),
        P(None, ("pool", "dev")),
        P(("pool", "dev"), None),
    )
    return jax.shard_map(
        per_device,
        mesh=mesh,
        in_specs=placed,
        out_specs=P(None, ("group", "pool", "dev"), None),
        check_vma=False,
    )
```

```python
import functools

import jax
import jax.numpy as jnp
from jax import lax
from jax.experimental import pallas as pl
from jax.experimental.pallas import tpu as pltpu
from jax.sharding import PartitionSpec as P

FF = 2048
CAP = 2
LINE = 4
PAIR = 2

route_scale = 2.5
MESH = pl.DeviceIdType.MESH
F32 = jnp.float32
BF16 = jnp.bfloat16


def dot(a, b):
    return jnp.dot(a, b, preferred_element_type=F32)


def dot_tn(a, b):
    return lax.dot_general(a, b, (((0,), (0,)), ((), ())), preferred_element_type=F32)


def dot_nt(a, b):
    return lax.dot_general(a, b, (((1,), (1,)), ((), ())), preferred_element_type=F32)


def kernel(
    tokens_hbm, routes, router, w_gate, w_up, w_down, out,
    tokens, gate_v, up_v, down_v, router_v, mine, theirs, rows, parts, from_x, from_up, from_down, sums,
    total_v, total_peer, logit_out, logit_in, logit_peer,
    load_sem, peer_send, peer_recv, row_recv, row_up, row_down, row_x,
    log_send, log_recv, x_send, x_recv, up_send, up_recv, down_send, down_recv,
):
    pool, dev = lax.axis_index("pool"), lax.axis_index("dev")
    chips = LINE * PAIR
    line, pair = dev // PAIR, dev % PAIR
    n_rows, width = tokens.shape
    half = width // 2
    block = n_rows // 2
    router_rows = router.shape[0]

    own_router = pltpu.make_async_copy(router, router_v.at[pool], load_sem.at[3])
    own_router.start()
    own_tokens = pltpu.make_async_copy(tokens_hbm, tokens, load_sem.at[4])
    own_tokens.start()
    loads = [
        pltpu.make_async_copy(w_gate, gate_v, load_sem.at[0]),
        pltpu.make_async_copy(w_up, up_v, load_sem.at[1]),
        pltpu.make_async_copy(w_down, down_v, load_sem.at[2]),
    ]
    barrier = pltpu.get_barrier_semaphore()
    pl.semaphore_signal(barrier, inc=1, device_id={"pool": 1 - pool}, device_id_type=MESH)
    for step in range(1, chips):
        pl.semaphore_signal(
            barrier, inc=1, device_id={"dev": lax.rem(dev + step, chips)}, device_id_type=MESH
        )

    ids = jnp.concatenate([routes[0], routes[1]], axis=1)
    slot_no = lax.broadcasted_iota(jnp.int32, (8, n_rows), 0)
    row_no = lax.broadcasted_iota(jnp.int32, (8, n_rows), 1)
    place = (row_no // block == (slot_no % 4) // 2) & (slot_no // 4 == pool)
    r0 = lax.broadcasted_iota(jnp.int32, (n_rows, n_rows), 0)
    r1 = lax.broadcasted_iota(jnp.int32, (n_rows, n_rows), 1)
    earlier = ((r0 < r1) & (r0 // block == r1 // block)).astype(F32).astype(BF16)

    def select(expert):
        named = jnp.max((ids == expert).astype(F32), axis=0, keepdims=True)
        named = jnp.broadcast_to(named, (8, n_rows))
        count = dot(named.astype(BF16), earlier)
        hit = (named > 0.5) & place & (count == (slot_no % 2).astype(F32))
        return hit.astype(F32)

    def in_slots(sel):
        sel = sel.astype(BF16)
        left = dot(sel, tokens[:, :half])
        right = dot(sel, tokens[:, half:])
        return jnp.concatenate([left, right], axis=0).astype(BF16)

    sel_own, sel_other = select(pool), select(1 - pool)
    own_tokens.wait()
    own_router.wait()
    for load in loads:
        load.start()
    mine[...] = in_slots(sel_other)

    pl.semaphore_wait(barrier, chips)

    def to_peer(src, dst, k):
        return pltpu.make_async_remote_copy(
            src, dst, peer_send.at[k], peer_recv.at[k],
            device_id={"pool": 1 - pool}, device_id_type=MESH,
        )

    peer_rows = to_peer(mine, theirs, 0)
    peer_rows.start()
    peer_router = to_peer(router_v.at[pool], router_v.at[pool], 1)
    peer_router.start()
    own = in_slots(sel_own)
    peer_rows.wait_recv()
    rows[dev] = own + theirs[...]

    def row_copy(z, target, sems):
        c = z * PAIR + pair
        return pltpu.make_async_remote_copy(
            rows.at[c], rows.at[c], sems.at[z], row_recv.at[c],
            device_id={"dev": target}, device_id_type=MESH,
        )

    def row_wait(c):
        pltpu.make_async_copy(rows.at[c], rows.at[c], row_recv.at[c]).wait()

    across = line * PAIR + 1 - pair

    @pl.when(line < LINE - 1)
    def _():
        row_copy(line, dev + PAIR, row_up).start()

    @pl.when(line > 0)
    def _():
        row_copy(line, dev - PAIR, row_down).start()

    row_copy(line, across, row_x).start()
    for d in range(1, LINE):
        @pl.when(line - d >= 0)
        def _():
            z = line - d
            row_wait(z * PAIR + pair)

            @pl.when(line < LINE - 1)
            def _():
                row_copy(z, dev + PAIR, row_up).start()

            row_copy(z, across, row_x).start()

        @pl.when(line + d < LINE)
        def _():
            z = line + d
            row_wait(z * PAIR + pair)

            @pl.when(line > 0)
            def _():
                row_copy(z, dev - PAIR, row_down).start()

            row_copy(z, across, row_x).start()

    for z in range(LINE):
        row_wait(z * PAIR + 1 - pair)
    peer_router.wait_recv()
    for load in loads:
        load.wait()

    tile = half // 4
    hid = gate_v.shape[1]

    def project(side):
        def body(k, carry):
            g, u, l = carry
            at = pl.multiple_of(k * tile, 128)
            deep = pl.multiple_of(side * half + k * tile, 128)
            a = rows[:, :, pl.ds(at, tile)].reshape(chips * 16, tile)
            r = router_v[:, :, pl.ds(deep, tile)].reshape(2 * router_rows, tile)
            g = g + dot(a, gate_v[pl.ds(deep, tile), :])
            u = u + dot(a, up_v[pl.ds(deep, tile), :])
            l = l + dot_nt(a, r)
            return g, u, l

        zero = jnp.zeros((chips * 16, hid), F32)
        got = lax.fori_loop(
            0, 4, body, (zero, zero, jnp.zeros((chips * 16, 2 * router_rows), F32))
        )
        return [v.reshape(chips, 16, v.shape[1])[:, side * 8 : side * 8 + 8] for v in got]

    (gl, ul, ll), (gr, ur, lr) = project(0), project(1)
    gate, up = gl + gr, ul + ur
    hidden = (gate / (1.0 + jnp.exp(-gate)) * up).astype(F32).reshape(chips * 8, hid).astype(BF16)
    logit_out[:, :, 0 : 2 * router_rows] = ll + lr
    logit_out[:, :, 2 * router_rows :] = jnp.zeros((chips, 8, 128 - 2 * router_rows), F32)
    logit_in[dev] = logit_out[dev]

    def log_copy(step):
        to = lax.rem(dev + step, chips)
        return pltpu.make_async_remote_copy(
            logit_out.at[to], logit_in.at[dev], log_send.at[step], log_recv.at[dev],
            device_id={"dev": to}, device_id_type=MESH,
        )

    for step in range(1, chips):
        log_copy(step).start()

    def down(t, _):
        at = pl.multiple_of(t * tile, 128)
        left = dot(hidden, down_v[:, pl.ds(at, tile)]).reshape(chips, 8, tile)
        right = dot(hidden, down_v[:, pl.ds(pl.multiple_of(half + at, 128), tile)]).reshape(chips, 8, tile)
        parts[:, :, pl.ds(at, tile)] = jnp.concatenate([left, right], axis=1).astype(BF16)
        return 0

    lax.fori_loop(0, 4, down, 0)

    def x_copy(z):
        return pltpu.make_async_remote_copy(
            parts.at[z * PAIR + 1 - pair], from_x.at[z], x_send.at[z], x_recv.at[z],
            device_id={"dev": across}, device_id_type=MESH,
        )

    def up_copy(z):
        return pltpu.make_async_remote_copy(
            sums.at[z], from_up.at[z], up_send.at[z], up_recv.at[z],
            device_id={"dev": dev + PAIR}, device_id_type=MESH,
        )

    def down_copy(z):
        return pltpu.make_async_remote_copy(
            sums.at[z], from_down.at[z], down_send.at[z], down_recv.at[z],
            device_id={"dev": dev - PAIR}, device_id_type=MESH,
        )

    def each_far_first(act_up, act_down):
        for d in range(LINE - 1, 0, -1):
            @pl.when(line + d < LINE)
            def _():
                act_up(line + d)

            @pl.when(line - d >= 0)
            def _():
                act_down(line - d)

    each_far_first(lambda z: x_copy(z).start(), lambda z: x_copy(z).start())
    x_copy(line).start()

    def paired(z):
        x_copy(z).wait_recv()
        return parts[z * PAIR + pair].astype(F32) + from_x[z].astype(F32)

    def go_up(z):
        total = paired(z)
        sums[z] = total.astype(BF16)

        @pl.when(line > 0)
        def _():
            up_copy(z).wait_recv()
            sums[z] = (total + from_up[z].astype(F32)).astype(BF16)

        up_copy(z).start()

    def go_down(z):
        total = paired(z)
        sums[z] = total.astype(BF16)

        @pl.when(line < LINE - 1)
        def _():
            down_copy(z).wait_recv()
            sums[z] = (total + from_down[z].astype(F32)).astype(BF16)

        down_copy(z).start()

    each_far_first(go_up, go_down)
    total_v[...] = paired(line)

    for step in range(1, chips):
        c = lax.rem(dev + step, chips)
        pltpu.make_async_copy(logit_in.at[c], logit_in.at[c], log_recv.at[c]).wait()
    peer_logits = to_peer(logit_in, logit_peer, 2)
    peer_logits.start()

    @pl.when(line > 0)
    def _():
        up_copy(line).wait_recv()
        total_v[...] += from_up[line].astype(F32)

    @pl.when(line < LINE - 1)
    def _():
        down_copy(line).wait_recv()
        total_v[...] += from_down[line].astype(F32)

    peer_total = to_peer(total_v, total_peer, 3)
    peer_total.start()

    lane = lax.broadcasted_iota(jnp.int32, (8, 128), 1)
    id_bf16 = ids.astype(F32).astype(BF16)

    def weigh(sel, logits, expert):
        named = dot_nt(sel.astype(BF16), id_bf16)
        near = jnp.zeros((8, 128), F32)
        every = jnp.zeros((8, 128), F32)
        for s in range(chips):
            number = (lane // router_rows) * (chips * router_rows) + s * router_rows + lane % router_rows
            number = jnp.where(lane < 2 * router_rows, number, -1)
            score = 1.0 / (1.0 + jnp.exp(-logits[s]))
            near += jnp.where(number == expert, score, 0.0)
            match = number.astype(F32) == named[:, 0:1]
            for k in range(1, ids.shape[0]):
                match |= number.astype(F32) == named[:, k : k + 1]
            every += jnp.where(match, score, 0.0)
        near = jnp.sum(near, axis=1, keepdims=True)
        every = jnp.sum(every, axis=1, keepdims=True)
        return route_scale * near / every

    def split(total, weight):
        j = lax.broadcasted_iota(jnp.int32, (8, 1), 0)
        both = []
        for side in range(2):
            v = jnp.where(j // 4 == pool, total[side * 8 : side * 8 + 8] * weight, 0.0)
            hi = v.astype(BF16).astype(F32)
            both.append(jnp.concatenate([hi, v - hi], axis=0).astype(BF16))
        return both

    own_weight = weigh(sel_own, logit_in, pool)
    own_left, own_right = split(total_v[...], own_weight)
    peer_logits.wait_recv()
    other_weight = weigh(sel_other, logit_peer, 1 - pool)
    peer_total.wait_recv()
    other_left, other_right = split(total_peer[...], other_weight)
    mixing = jnp.concatenate([sel_own, sel_own, sel_other, sel_other], axis=0).astype(BF16)
    out[:, :half] = dot_tn(mixing, jnp.concatenate([own_left, other_left], axis=0)).astype(BF16)
    out[:, half:] = dot_tn(mixing, jnp.concatenate([own_right, other_right], axis=0)).astype(BF16)

    for copy in (peer_rows, peer_router, peer_logits, peer_total):
        copy.wait_send()
    for z in range(LINE):
        row_copy(z, across, row_x).wait_send()
        x_copy(z).wait_send()

        @pl.when((line < LINE - 1) & (z <= line))
        def _():
            row_copy(z, dev + PAIR, row_up).wait_send()

        @pl.when((line > 0) & (z >= line))
        def _():
            row_copy(z, dev - PAIR, row_down).wait_send()

        @pl.when(z > line)
        def _():
            up_copy(z).wait_send()

        @pl.when(z < line)
        def _():
            down_copy(z).wait_send()

    for step in range(1, chips):
        log_copy(step).wait_send()


def fused(tokens, routes, router, w_gate, w_up, w_down):
    batches, block, width = tokens.shape
    half = width // 2
    chips = LINE * PAIR
    n_rows = batches * block
    vmem = pl.BlockSpec(memory_space=pltpu.VMEM)
    hbm = pl.BlockSpec(memory_space=pltpu.HBM)
    dma = pltpu.SemaphoreType.DMA
    out = pl.pallas_call(
        kernel,
        out_shape=jax.ShapeDtypeStruct((n_rows, width), BF16),
        in_specs=[hbm, vmem, hbm, hbm, hbm, hbm],
        out_specs=vmem,
        scratch_shapes=[
            pltpu.VMEM((n_rows, width), BF16),
            pltpu.VMEM(w_gate.shape, BF16),
            pltpu.VMEM(w_up.shape, BF16),
            pltpu.VMEM(w_down.shape, BF16),
            pltpu.VMEM((2, router.shape[0], width), BF16),
            pltpu.VMEM((16, half), BF16),
            pltpu.VMEM((16, half), BF16),
            pltpu.VMEM((chips, 16, half), BF16),
            pltpu.VMEM((chips, 16, half), BF16),
            pltpu.VMEM((LINE, 16, half), BF16),
            pltpu.VMEM((LINE, 16, half), BF16),
            pltpu.VMEM((LINE, 16, half), BF16),
            pltpu.VMEM((LINE, 16, half), BF16),
            pltpu.VMEM((16, half), F32),
            pltpu.VMEM((16, half), F32),
            pltpu.VMEM((chips, 8, 128), F32),
            pltpu.VMEM((chips, 8, 128), F32),
            pltpu.VMEM((chips, 8, 128), F32),
            dma((5,)), dma((4,)), dma((4,)), dma((chips,)), dma((LINE,)), dma((LINE,)), dma((LINE,)),
            dma((chips,)), dma((chips,)), dma((LINE,)), dma((LINE,)), dma((LINE,)), dma((LINE,)),
            dma((LINE,)), dma((LINE,)),
        ],
        compiler_params=pltpu.CompilerParams(
            collective_id=0, has_side_effects=True, vmem_limit_bytes=(64 << 20) - (256 << 10)
        ),
    )(tokens.reshape(n_rows, width), routes.transpose(0, 2, 1), router, w_gate, w_up, w_down)
    return out.reshape(tokens.shape)


def spread(tokens, routes, router, w_gate, w_up, w_down):
    groups = lax.axis_size(("pool", "dev"))
    batches = tokens.shape[0]
    model_width = tokens.shape[2]
    hidden_width = w_gate.shape[1]
    slices = FF // hidden_width
    experts_win = groups // slices
    capacity = CAP
    logits = jnp.einsum(
        "mrd,ed->mre",
        tokens,
        lax.all_gather(router, ("pool", "dev"), axis=0, tiled=True),
        preferred_element_type=jnp.float32,
    )
    scores = jax.nn.sigmoid(logits)
    expert_ids = jnp.arange(logits.shape[2], dtype=jnp.int32)
    picked = routes[..., None] == expert_ids
    chosen = jnp.sum(jnp.where(picked, scores[:, :, None, :], 0.0), axis=-1)
    weights = route_scale * chosen / jnp.sum(chosen, axis=-1, keepdims=True)
    window = picked[..., :experts_win]
    route_weight = jnp.sum(jnp.where(window, weights[..., None], 0.0), axis=2)
    routed = jnp.any(window, axis=2).astype(jnp.int32)
    position = jnp.cumsum(routed, axis=1) - 1
    slot_ids = jnp.arange(capacity, dtype=jnp.int32)
    selector = (routed[..., None] == 1) & (position[..., None] == slot_ids)
    slot_rows = jnp.einsum(
        "mrec,mrd->mecd", selector.astype(jnp.bfloat16), tokens, preferred_element_type=jnp.float32
    ).astype(jnp.bfloat16)
    outgoing = jnp.broadcast_to(
        slot_rows[:, :, None], (batches, experts_win, slices, capacity, model_width)
    )
    outgoing = outgoing.reshape(batches, groups, capacity, model_width)
    arrived = lax.all_to_all(outgoing, ("pool", "dev"), split_axis=1, concat_axis=1, tiled=True)
    flat_rows = arrived.reshape(-1, model_width)
    gate_proj = jnp.dot(flat_rows, w_gate, preferred_element_type=jnp.float32)
    up_proj = jnp.dot(flat_rows, w_up, preferred_element_type=jnp.float32)
    hidden = (jax.nn.silu(gate_proj) * up_proj).astype(jnp.bfloat16)
    partial_value = jnp.dot(hidden, w_down, preferred_element_type=jnp.float32).astype(jnp.bfloat16)
    send_partial_value = partial_value.reshape(arrived.shape)
    returned = lax.all_to_all(
        send_partial_value, ("pool", "dev"), split_axis=1, concat_axis=1, tiled=True
    )
    returned = returned.reshape(batches, experts_win, slices, capacity, model_width)
    expert_out = jnp.sum(returned, axis=2, dtype=jnp.float32)
    mixing = selector.astype(jnp.float32) * route_weight[..., None]
    combined = jnp.einsum("mrec,mecd->mrd", mixing, expert_out, precision=lax.Precision.HIGHEST)
    return combined.astype(jnp.bfloat16)


def solution(mesh):
    shape = dict(mesh.shape)
    per_device = fused if (shape["pool"], shape["dev"]) == (2, LINE * PAIR) else spread
    placed = (
        P(None, ("group", "pool", "dev"), None),
        P(None, ("group", "pool", "dev"), None),
        P(("pool", "dev"), None),
        P(None, ("pool", "dev")),
        P(None, ("pool", "dev")),
        P(("pool", "dev"), None),
    )
    return jax.shard_map(
        per_device,
        mesh=mesh,
        in_specs=placed,
        out_specs=P(None, ("group", "pool", "dev"), None),
        check_vma=False,
    )
```

```python
import functools

import jax
import jax.numpy as jnp
from jax import lax
from jax.experimental import pallas as pl
from jax.experimental.pallas import tpu as pltpu
from jax.sharding import PartitionSpec as P

FF = 2048
CAP = 2
LINE = 4
PAIR = 2
PIECES = 2

route_scale = 2.5
MESH = pl.DeviceIdType.MESH
F32 = jnp.float32
BF16 = jnp.bfloat16


def dot(a, b):
    return jnp.dot(a, b, preferred_element_type=F32)


def dot_tn(a, b):
    return lax.dot_general(a, b, (((0,), (0,)), ((), ())), preferred_element_type=F32)


def dot_nt(a, b):
    return lax.dot_general(a, b, (((1,), (1,)), ((), ())), preferred_element_type=F32)


def kernel(
    tokens_hbm, routes, router, w_gate, w_up, w_down, values, mixing,
    tokens, gate_v, up_v, down_v, router_v, mine, theirs, rows, parts, from_x, from_up, from_down, sums,
    total_v, total_peer, logit_out, logit_in, logit_peer,
    load_sem, peer_send, peer_recv, row_recv, row_up, row_down, row_x,
    log_send, log_recv, x_send, x_recv, up_send, up_recv, down_send, down_recv,
):
    pool, dev = lax.axis_index("pool"), lax.axis_index("dev")
    chips = LINE * PAIR
    line, pair = dev // PAIR, dev % PAIR
    n_rows, width = tokens.shape
    half = width // 2
    piece = half // PIECES
    block = n_rows // 2
    router_rows = router.shape[0]

    own_router = pltpu.make_async_copy(router, router_v.at[pool], load_sem.at[3])
    own_router.start()
    own_tokens = pltpu.make_async_copy(tokens_hbm, tokens, load_sem.at[4])
    own_tokens.start()
    loads = [
        pltpu.make_async_copy(w_gate, gate_v, load_sem.at[0]),
        pltpu.make_async_copy(w_up, up_v, load_sem.at[1]),
        pltpu.make_async_copy(w_down, down_v, load_sem.at[2]),
    ]
    barrier = pltpu.get_barrier_semaphore()
    pl.semaphore_signal(barrier, inc=1, device_id={"pool": 1 - pool}, device_id_type=MESH)
    for step in range(1, chips):
        pl.semaphore_signal(
            barrier, inc=1, device_id={"dev": lax.rem(dev + step, chips)}, device_id_type=MESH
        )

    ids = jnp.concatenate([routes[0], routes[1]], axis=1)
    slot_no = lax.broadcasted_iota(jnp.int32, (8, n_rows), 0)
    row_no = lax.broadcasted_iota(jnp.int32, (8, n_rows), 1)
    place = (row_no // block == (slot_no % 4) // 2) & (slot_no // 4 == pool)
    r0 = lax.broadcasted_iota(jnp.int32, (n_rows, n_rows), 0)
    r1 = lax.broadcasted_iota(jnp.int32, (n_rows, n_rows), 1)
    earlier = ((r0 < r1) & (r0 // block == r1 // block)).astype(F32).astype(BF16)

    def select(expert):
        named = jnp.max((ids == expert).astype(F32), axis=0, keepdims=True)
        named = jnp.broadcast_to(named, (8, n_rows))
        count = dot(named.astype(BF16), earlier)
        hit = (named > 0.5) & place & (count == (slot_no % 2).astype(F32))
        return hit.astype(F32)

    def in_slots(sel, p):
        sel = sel.astype(BF16)
        left = dot(sel, tokens[:, p * piece : (p + 1) * piece])
        right = dot(sel, tokens[:, half + p * piece : half + (p + 1) * piece])
        return jnp.concatenate([left, right], axis=0).astype(BF16)

    sel_own, sel_other = select(pool), select(1 - pool)
    own_tokens.wait()
    own_router.wait()
    for load in loads:
        load.start()
    for p in range(PIECES):
        mine[p] = in_slots(sel_other, p)

    pl.semaphore_wait(barrier, chips)

    def to_peer(src, dst, k):
        return pltpu.make_async_remote_copy(
            src, dst, peer_send.at[k], peer_recv.at[k],
            device_id={"pool": 1 - pool}, device_id_type=MESH,
        )

    peer_rows = [to_peer(mine.at[p], theirs.at[p], p) for p in range(PIECES)]
    for copy in peer_rows:
        copy.start()
    peer_router = to_peer(router_v.at[pool], router_v.at[pool], 2 * PIECES)
    peer_router.start()

    def row_copy(p, z, target, sems):
        c = z * PAIR + pair
        return pltpu.make_async_remote_copy(
            rows.at[p, c], rows.at[p, c], sems.at[p, z], row_recv.at[p, c],
            device_id={"dev": target}, device_id_type=MESH,
        )

    def row_wait(p, c):
        pltpu.make_async_copy(rows.at[p, c], rows.at[p, c], row_recv.at[p, c]).wait()

    across = line * PAIR + 1 - pair
    for p in range(PIECES):
        own = in_slots(sel_own, p)
        peer_rows[p].wait_recv()
        rows[p, dev] = own + theirs[p]

        @pl.when(line < LINE - 1)
        def _():
            row_copy(p, line, dev + PAIR, row_up).start()

        @pl.when(line > 0)
        def _():
            row_copy(p, line, dev - PAIR, row_down).start()

        row_copy(p, line, across, row_x).start()

    for d in range(1, LINE):
        for p in range(PIECES):
            @pl.when(line - d >= 0)
            def _():
                z = line - d
                row_wait(p, z * PAIR + pair)

                @pl.when(line < LINE - 1)
                def _():
                    row_copy(p, z, dev + PAIR, row_up).start()

                row_copy(p, z, across, row_x).start()

            @pl.when(line + d < LINE)
            def _():
                z = line + d
                row_wait(p, z * PAIR + pair)

                @pl.when(line > 0)
                def _():
                    row_copy(p, z, dev - PAIR, row_down).start()

                row_copy(p, z, across, row_x).start()

    peer_router.wait_recv()
    for load in loads:
        load.wait()
    for p in range(PIECES):
        for z in range(LINE):
            row_wait(p, z * PAIR + 1 - pair)

    hid = gate_v.shape[1]

    def project(side):
        def body(k, carry):
            g, u, l = carry
            deep = pl.multiple_of(side * half + k * piece, 128)
            a = rows[k].reshape(chips * 16, piece)
            r = router_v[:, :, pl.ds(deep, piece)].reshape(2 * router_rows, piece)
            g = g + dot(a, gate_v[pl.ds(deep, piece), :])
            u = u + dot(a, up_v[pl.ds(deep, piece), :])
            l = l + dot_nt(a, r)
            return g, u, l

        zero = jnp.zeros((chips * 16, hid), F32)
        got = lax.fori_loop(
            0, PIECES, body, (zero, zero, jnp.zeros((chips * 16, 2 * router_rows), F32))
        )
        return [v.reshape(chips, 16, v.shape[1])[:, side * 8 : side * 8 + 8] for v in got]

    (gl, ul, ll), (gr, ur, lr) = project(0), project(1)
    gate, up = gl + gr, ul + ur
    hidden = (gate / (1.0 + jnp.exp(-gate)) * up).astype(F32).reshape(chips * 8, hid).astype(BF16)
    logit_out[:, :, 0 : 2 * router_rows] = ll + lr
    logit_out[:, :, 2 * router_rows :] = jnp.zeros((chips, 8, 128 - 2 * router_rows), F32)
    logit_in[dev] = logit_out[dev]

    def log_copy(step):
        to = lax.rem(dev + step, chips)
        return pltpu.make_async_remote_copy(
            logit_out.at[to], logit_in.at[dev], log_send.at[step], log_recv.at[dev],
            device_id={"dev": to}, device_id_type=MESH,
        )

    for step in range(1, chips):
        log_copy(step).start()

    def x_copy(p, z):
        return pltpu.make_async_remote_copy(
            parts.at[p, z * PAIR + 1 - pair], from_x.at[p, z], x_send.at[p, z], x_recv.at[p, z],
            device_id={"dev": across}, device_id_type=MESH,
        )

    def up_copy(p, z):
        return pltpu.make_async_remote_copy(
            sums.at[p, z], from_up.at[p, z], up_send.at[p, z], up_recv.at[p, z],
            device_id={"dev": dev + PAIR}, device_id_type=MESH,
        )

    def down_copy(p, z):
        return pltpu.make_async_remote_copy(
            sums.at[p, z], from_down.at[p, z], down_send.at[p, z], down_recv.at[p, z],
            device_id={"dev": dev - PAIR}, device_id_type=MESH,
        )

    def each_far_first(act_up, act_down):
        for d in range(LINE - 1, 0, -1):
            @pl.when(line + d < LINE)
            def _():
                act_up(line + d)

            @pl.when(line - d >= 0)
            def _():
                act_down(line - d)

    for p in range(PIECES):
        left = dot(hidden, down_v[:, p * piece : (p + 1) * piece])
        right = dot(hidden, down_v[:, half + p * piece : half + (p + 1) * piece])
        both = [left.reshape(chips, 8, piece), right.reshape(chips, 8, piece)]
        parts[p] = jnp.concatenate(both, axis=1).astype(BF16)
        each_far_first(lambda z: x_copy(p, z).start(), lambda z: x_copy(p, z).start())
        x_copy(p, line).start()

    lane = lax.broadcasted_iota(jnp.int32, (8, 128), 1)
    id_bf16 = ids.astype(F32).astype(BF16)

    def weigh(sel, logits, expert):
        named = dot_nt(sel.astype(BF16), id_bf16)
        near = jnp.zeros((8, 128), F32)
        every = jnp.zeros((8, 128), F32)
        for s in range(chips):
            number = (lane // router_rows) * (chips * router_rows) + s * router_rows + lane % router_rows
            number = jnp.where(lane < 2 * router_rows, number, -1)
            score = 1.0 / (1.0 + jnp.exp(-logits[s]))
            near += jnp.where(number == expert, score, 0.0)
            match = number.astype(F32) == named[:, 0:1]
            for k in range(1, ids.shape[0]):
                match |= number.astype(F32) == named[:, k : k + 1]
            every += jnp.where(match, score, 0.0)
        near = jnp.sum(near, axis=1, keepdims=True)
        every = jnp.sum(every, axis=1, keepdims=True)
        return route_scale * near / every

    def split(total, weight):
        j = lax.broadcasted_iota(jnp.int32, (8, 1), 0)
        both = []
        for side in range(2):
            v = jnp.where(j // 4 == pool, total[side * 8 : side * 8 + 8] * weight, 0.0)
            hi = v.astype(BF16).astype(F32)
            both.append(jnp.concatenate([hi, v - hi], axis=0).astype(BF16))
        return both

    for step in range(1, chips):
        c = lax.rem(dev + step, chips)
        pltpu.make_async_copy(logit_in.at[c], logit_in.at[c], log_recv.at[c]).wait()
    peer_logits = to_peer(logit_in, logit_peer, 2 * PIECES + 1)
    peer_logits.start()
    own_weight = weigh(sel_own, logit_in, pool)

    def paired(p, z):
        x_copy(p, z).wait_recv()
        return parts[p, z * PAIR + pair].astype(F32) + from_x[p, z].astype(F32)

    def go_up(p, z):
        total = paired(p, z)

        @pl.when(line > 0)
        def _():
            up_copy(p, z).wait_recv()
            sums[p, z] = (total + from_up[p, z].astype(F32)).astype(BF16)

        @pl.when(line == 0)
        def _():
            sums[p, z] = total.astype(BF16)

        up_copy(p, z).start()

    def go_down(p, z):
        total = paired(p, z)

        @pl.when(line < LINE - 1)
        def _():
            down_copy(p, z).wait_recv()
            sums[p, z] = (total + from_down[p, z].astype(F32)).astype(BF16)

        @pl.when(line == LINE - 1)
        def _():
            sums[p, z] = total.astype(BF16)

        down_copy(p, z).start()

    peer_total = [
        to_peer(total_v.at[p], total_peer.at[p], PIECES + p) for p in range(PIECES)
    ]

    def finish(p):
        total_v[p] = paired(p, line)

        @pl.when(line > 0)
        def _():
            up_copy(p, line).wait_recv()
            total_v[p] += from_up[p, line].astype(F32)

        @pl.when(line < LINE - 1)
        def _():
            down_copy(p, line).wait_recv()
            total_v[p] += from_down[p, line].astype(F32)

        peer_total[p].start()

    for p in range(PIECES):
        each_far_first(lambda z: go_up(p, z), lambda z: go_down(p, z))
        if p:
            finish(p - 1)
    peer_logits.wait_recv()
    other_weight = weigh(sel_other, logit_peer, 1 - pool)

    def mix(sel, weight):
        return jnp.where(sel > 0.5, jnp.broadcast_to(weight * 0.0 + 1.0, sel.shape), 0.0)

    own_mix, other_mix = mix(sel_own, own_weight), mix(sel_other, other_weight)
    mixing[...] = jnp.concatenate([own_mix, own_mix, other_mix, other_mix], axis=0).astype(BF16)
    own_weight = jnp.where(own_weight == own_weight, own_weight, 0.0)
    other_weight = jnp.where(other_weight == other_weight, other_weight, 0.0)
    finish(PIECES - 1)

    def give(p, total, weight, first):
        left, right = split(total, weight)
        values[first : first + 16, p * piece : (p + 1) * piece] = left
        values[first : first + 16, half + p * piece : half + (p + 1) * piece] = right

    for p in range(PIECES):
        give(p, total_v[p], own_weight, 0)
    for p in range(PIECES):
        peer_total[p].wait_recv()
        give(p, total_peer[p], other_weight, 16)

    for copy in (*peer_rows, peer_router, peer_logits, *peer_total):
        copy.wait_send()
    for p, z in [(p, z) for p in range(PIECES) for z in range(LINE)]:
        row_copy(p, z, across, row_x).wait_send()
        x_copy(p, z).wait_send()

        @pl.when((line < LINE - 1) & (z <= line))
        def _():
            row_copy(p, z, dev + PAIR, row_up).wait_send()

        @pl.when((line > 0) & (z >= line))
        def _():
            row_copy(p, z, dev - PAIR, row_down).wait_send()

        @pl.when(z > line)
        def _():
            up_copy(p, z).wait_send()

        @pl.when(z < line)
        def _():
            down_copy(p, z).wait_send()

    for step in range(1, chips):
        log_copy(step).wait_send()


def fused(tokens, routes, router, w_gate, w_up, w_down):
    batches, block, width = tokens.shape
    half = width // 2
    chips = LINE * PAIR
    n_rows = batches * block
    vmem = pl.BlockSpec(memory_space=pltpu.VMEM)
    hbm = pl.BlockSpec(memory_space=pltpu.HBM)
    dma = pltpu.SemaphoreType.DMA
    values, mixing = pl.pallas_call(
        kernel,
        out_shape=(jax.ShapeDtypeStruct((32, width), BF16), jax.ShapeDtypeStruct((32, n_rows), BF16)),
        in_specs=[hbm, vmem, hbm, hbm, hbm, hbm],
        out_specs=(vmem, vmem),
        scratch_shapes=[
            pltpu.VMEM((n_rows, width), BF16),
            pltpu.VMEM(w_gate.shape, BF16),
            pltpu.VMEM(w_up.shape, BF16),
            pltpu.VMEM(w_down.shape, BF16),
            pltpu.VMEM((2, router.shape[0], width), BF16),
            pltpu.VMEM((PIECES, 16, half // PIECES), BF16),
            pltpu.VMEM((PIECES, 16, half // PIECES), BF16),
            pltpu.VMEM((PIECES, chips, 16, half // PIECES), BF16),
            pltpu.VMEM((PIECES, chips, 16, half // PIECES), BF16),
            pltpu.VMEM((PIECES, LINE, 16, half // PIECES), BF16),
            pltpu.VMEM((PIECES, LINE, 16, half // PIECES), BF16),
            pltpu.VMEM((PIECES, LINE, 16, half // PIECES), BF16),
            pltpu.VMEM((PIECES, LINE, 16, half // PIECES), BF16),
            pltpu.VMEM((PIECES, 16, half // PIECES), F32),
            pltpu.VMEM((PIECES, 16, half // PIECES), F32),
            pltpu.VMEM((chips, 8, 128), F32),
            pltpu.VMEM((chips, 8, 128), F32),
            pltpu.VMEM((chips, 8, 128), F32),
            dma((5,)), dma((2 * PIECES + 2,)), dma((2 * PIECES + 2,)), dma((PIECES, chips)),
            dma((PIECES, LINE)), dma((PIECES, LINE)), dma((PIECES, LINE)),
            dma((chips,)), dma((chips,)), dma((PIECES, LINE)), dma((PIECES, LINE)),
            dma((PIECES, LINE)), dma((PIECES, LINE)), dma((PIECES, LINE)), dma((PIECES, LINE)),
        ],
        compiler_params=pltpu.CompilerParams(
            collective_id=0, has_side_effects=True, vmem_limit_bytes=(64 << 20) - (256 << 10)
        ),
    )(tokens.reshape(n_rows, width), routes.transpose(0, 2, 1), router, w_gate, w_up, w_down)
    return dot_tn(mixing, values).astype(BF16).reshape(tokens.shape)


def spread(tokens, routes, router, w_gate, w_up, w_down):
    groups = lax.axis_size(("pool", "dev"))
    batches = tokens.shape[0]
    model_width = tokens.shape[2]
    hidden_width = w_gate.shape[1]
    slices = FF // hidden_width
    experts_win = groups // slices
    capacity = CAP
    logits = jnp.einsum(
        "mrd,ed->mre",
        tokens,
        lax.all_gather(router, ("pool", "dev"), axis=0, tiled=True),
        preferred_element_type=jnp.float32,
    )
    scores = jax.nn.sigmoid(logits)
    expert_ids = jnp.arange(logits.shape[2], dtype=jnp.int32)
    picked = routes[..., None] == expert_ids
    chosen = jnp.sum(jnp.where(picked, scores[:, :, None, :], 0.0), axis=-1)
    weights = route_scale * chosen / jnp.sum(chosen, axis=-1, keepdims=True)
    window = picked[..., :experts_win]
    route_weight = jnp.sum(jnp.where(window, weights[..., None], 0.0), axis=2)
    routed = jnp.any(window, axis=2).astype(jnp.int32)
    position = jnp.cumsum(routed, axis=1) - 1
    slot_ids = jnp.arange(capacity, dtype=jnp.int32)
    selector = (routed[..., None] == 1) & (position[..., None] == slot_ids)
    slot_rows = jnp.einsum(
        "mrec,mrd->mecd", selector.astype(jnp.bfloat16), tokens, preferred_element_type=jnp.float32
    ).astype(jnp.bfloat16)
    outgoing = jnp.broadcast_to(
        slot_rows[:, :, None], (batches, experts_win, slices, capacity, model_width)
    )
    outgoing = outgoing.reshape(batches, groups, capacity, model_width)
    arrived = lax.all_to_all(outgoing, ("pool", "dev"), split_axis=1, concat_axis=1, tiled=True)
    flat_rows = arrived.reshape(-1, model_width)
    gate_proj = jnp.dot(flat_rows, w_gate, preferred_element_type=jnp.float32)
    up_proj = jnp.dot(flat_rows, w_up, preferred_element_type=jnp.float32)
    hidden = (jax.nn.silu(gate_proj) * up_proj).astype(jnp.bfloat16)
    partial_value = jnp.dot(hidden, w_down, preferred_element_type=jnp.float32).astype(jnp.bfloat16)
    send_partial_value = partial_value.reshape(arrived.shape)
    returned = lax.all_to_all(
        send_partial_value, ("pool", "dev"), split_axis=1, concat_axis=1, tiled=True
    )
    returned = returned.reshape(batches, experts_win, slices, capacity, model_width)
    expert_out = jnp.sum(returned, axis=2, dtype=jnp.float32)
    mixing = selector.astype(jnp.float32) * route_weight[..., None]
    combined = jnp.einsum("mrec,mecd->mrd", mixing, expert_out, precision=lax.Precision.HIGHEST)
    return combined.astype(jnp.bfloat16)


def solution(mesh):
    shape = dict(mesh.shape)
    per_device = fused if (shape["pool"], shape["dev"]) == (2, LINE * PAIR) else spread
    placed = (
        P(None, ("group", "pool", "dev"), None),
        P(None, ("group", "pool", "dev"), None),
        P(("pool", "dev"), None),
        P(None, ("pool", "dev")),
        P(None, ("pool", "dev")),
        P(("pool", "dev"), None),
    )
    return jax.shard_map(
        per_device,
        mesh=mesh,
        in_specs=placed,
        out_specs=P(None, ("group", "pool", "dev"), None),
        check_vma=False,
    )
```

```python
import functools

import jax
import jax.numpy as jnp
from jax import lax
from jax.experimental import pallas as pl
from jax.experimental.pallas import tpu as pltpu
from jax.sharding import PartitionSpec as P

FF = 2048
CAP = 2
LINE = 4
PAIR = 2
PIECES = 2

route_scale = 2.5
MESH = pl.DeviceIdType.MESH
F32 = jnp.float32
BF16 = jnp.bfloat16


def dot(a, b):
    return jnp.dot(a, b, preferred_element_type=F32)


def dot_tn(a, b):
    return lax.dot_general(a, b, (((0,), (0,)), ((), ())), preferred_element_type=F32)


def dot_nt(a, b):
    return lax.dot_general(a, b, (((1,), (1,)), ((), ())), preferred_element_type=F32)


def kernel(
    tokens_hbm, routes, router, w_gate, w_up, w_down, out,
    tokens, values, gate_v, up_v, down_v, router_v, mine, theirs, rows, parts, from_x, from_up, from_down, sums,
    total_v, total_peer, logit_out, logit_in, logit_peer,
    load_sem, peer_send, peer_recv, row_recv, row_up, row_down, row_x,
    log_send, log_recv, x_send, x_recv, up_send, up_recv, down_send, down_recv,
):
    pool, dev = lax.axis_index("pool"), lax.axis_index("dev")
    chips = LINE * PAIR
    line, pair = dev // PAIR, dev % PAIR
    n_rows, width = tokens.shape
    half = width // 2
    piece = half // PIECES
    block = n_rows // 2
    router_rows = router.shape[0]

    own_router = pltpu.make_async_copy(router, router_v.at[pool], load_sem.at[3])
    own_router.start()
    own_tokens = pltpu.make_async_copy(tokens_hbm, tokens, load_sem.at[4])
    own_tokens.start()
    loads = [
        pltpu.make_async_copy(w_gate, gate_v, load_sem.at[0]),
        pltpu.make_async_copy(w_up, up_v, load_sem.at[1]),
        pltpu.make_async_copy(w_down, down_v, load_sem.at[2]),
    ]
    barrier = pltpu.get_barrier_semaphore()
    pl.semaphore_signal(barrier, inc=1, device_id={"pool": 1 - pool}, device_id_type=MESH)
    for step in range(1, chips):
        pl.semaphore_signal(
            barrier, inc=1, device_id={"dev": lax.rem(dev + step, chips)}, device_id_type=MESH
        )

    ids = jnp.concatenate([routes[0], routes[1]], axis=1)
    slot_no = lax.broadcasted_iota(jnp.int32, (8, n_rows), 0)
    row_no = lax.broadcasted_iota(jnp.int32, (8, n_rows), 1)
    place = (row_no // block == (slot_no % 4) // 2) & (slot_no // 4 == pool)
    r0 = lax.broadcasted_iota(jnp.int32, (n_rows, n_rows), 0)
    r1 = lax.broadcasted_iota(jnp.int32, (n_rows, n_rows), 1)
    earlier = ((r0 < r1) & (r0 // block == r1 // block)).astype(F32).astype(BF16)

    def select(expert):
        named = jnp.max((ids == expert).astype(F32), axis=0, keepdims=True)
        named = jnp.broadcast_to(named, (8, n_rows))
        count = dot(named.astype(BF16), earlier)
        hit = (named > 0.5) & place & (count == (slot_no % 2).astype(F32))
        return hit.astype(F32)

    def in_slots(sel, p):
        sel = sel.astype(BF16)
        left = dot(sel, tokens[:, p * piece : (p + 1) * piece])
        right = dot(sel, tokens[:, half + p * piece : half + (p + 1) * piece])
        return jnp.concatenate([left, right], axis=0).astype(BF16)

    sel_own, sel_other = select(pool), select(1 - pool)
    own_tokens.wait()
    own_router.wait()
    for load in loads:
        load.start()
    for p in range(PIECES):
        mine[p] = in_slots(sel_other, p)

    pl.semaphore_wait(barrier, chips)

    def to_peer(src, dst, k):
        return pltpu.make_async_remote_copy(
            src, dst, peer_send.at[k], peer_recv.at[k],
            device_id={"pool": 1 - pool}, device_id_type=MESH,
        )

    peer_rows = [to_peer(mine.at[p], theirs.at[p], p) for p in range(PIECES)]
    for copy in peer_rows:
        copy.start()
    peer_router = to_peer(router_v.at[pool], router_v.at[pool], 2 * PIECES)
    peer_router.start()

    def row_copy(p, z, target, sems):
        c = z * PAIR + pair
        return pltpu.make_async_remote_copy(
            rows.at[p, c], rows.at[p, c], sems.at[p, z], row_recv.at[p, c],
            device_id={"dev": target}, device_id_type=MESH,
        )

    def row_wait(p, c):
        pltpu.make_async_copy(rows.at[p, c], rows.at[p, c], row_recv.at[p, c]).wait()

    across = line * PAIR + 1 - pair
    for p in range(PIECES):
        own = in_slots(sel_own, p)
        peer_rows[p].wait_recv()
        rows[p, dev] = own + theirs[p]

        @pl.when(line < LINE - 1)
        def _():
            row_copy(p, line, dev + PAIR, row_up).start()

        @pl.when(line > 0)
        def _():
            row_copy(p, line, dev - PAIR, row_down).start()

        row_copy(p, line, across, row_x).start()

    for d in range(1, LINE):
        for p in range(PIECES):
            @pl.when(line - d >= 0)
            def _():
                z = line - d
                row_wait(p, z * PAIR + pair)

                @pl.when(line < LINE - 1)
                def _():
                    row_copy(p, z, dev + PAIR, row_up).start()

                row_copy(p, z, across, row_x).start()

            @pl.when(line + d < LINE)
            def _():
                z = line + d
                row_wait(p, z * PAIR + pair)

                @pl.when(line > 0)
                def _():
                    row_copy(p, z, dev - PAIR, row_down).start()

                row_copy(p, z, across, row_x).start()

    peer_router.wait_recv()
    for load in loads:
        load.wait()
    for p in range(PIECES):
        for z in range(LINE):
            row_wait(p, z * PAIR + 1 - pair)

    hid = gate_v.shape[1]

    def project(side):
        def body(k, carry):
            g, u, l = carry
            deep = pl.multiple_of(side * half + k * piece, 128)
            a = rows[k].reshape(chips * 16, piece)
            r = router_v[:, :, pl.ds(deep, piece)].reshape(2 * router_rows, piece)
            g = g + dot(a, gate_v[pl.ds(deep, piece), :])
            u = u + dot(a, up_v[pl.ds(deep, piece), :])
            l = l + dot_nt(a, r)
            return g, u, l

        zero = jnp.zeros((chips * 16, hid), F32)
        got = lax.fori_loop(
            0, PIECES, body, (zero, zero, jnp.zeros((chips * 16, 2 * router_rows), F32))
        )
        return [v.reshape(chips, 16, v.shape[1])[:, side * 8 : side * 8 + 8] for v in got]

    (gl, ul, ll), (gr, ur, lr) = project(0), project(1)
    gate, up = gl + gr, ul + ur
    hidden = (gate / (1.0 + jnp.exp(-gate)) * up).astype(F32).reshape(chips * 8, hid).astype(BF16)
    logit_out[:, :, 0 : 2 * router_rows] = ll + lr
    logit_out[:, :, 2 * router_rows :] = jnp.zeros((chips, 8, 128 - 2 * router_rows), F32)
    logit_in[dev] = logit_out[dev]

    def log_copy(step):
        to = lax.rem(dev + step, chips)
        return pltpu.make_async_remote_copy(
            logit_out.at[to], logit_in.at[dev], log_send.at[step], log_recv.at[dev],
            device_id={"dev": to}, device_id_type=MESH,
        )

    for step in range(1, chips):
        log_copy(step).start()

    def x_copy(p, z):
        return pltpu.make_async_remote_copy(
            parts.at[p, z * PAIR + 1 - pair], from_x.at[p, z], x_send.at[p, z], x_recv.at[p, z],
            device_id={"dev": across}, device_id_type=MESH,
        )

    def up_copy(p, z):
        return pltpu.make_async_remote_copy(
            sums.at[p, z], from_up.at[p, z], up_send.at[p, z], up_recv.at[p, z],
            device_id={"dev": dev + PAIR}, device_id_type=MESH,
        )

    def down_copy(p, z):
        return pltpu.make_async_remote_copy(
            sums.at[p, z], from_down.at[p, z], down_send.at[p, z], down_recv.at[p, z],
            device_id={"dev": dev - PAIR}, device_id_type=MESH,
        )

    def each_far_first(act_up, act_down):
        for d in range(LINE - 1, 0, -1):
            @pl.when(line + d < LINE)
            def _():
                act_up(line + d)

            @pl.when(line - d >= 0)
            def _():
                act_down(line - d)

    for p in range(PIECES):
        left = dot(hidden, down_v[:, p * piece : (p + 1) * piece])
        right = dot(hidden, down_v[:, half + p * piece : half + (p + 1) * piece])
        both = [left.reshape(chips, 8, piece), right.reshape(chips, 8, piece)]
        parts[p] = jnp.concatenate(both, axis=1).astype(BF16)
        each_far_first(lambda z: x_copy(p, z).start(), lambda z: x_copy(p, z).start())
        x_copy(p, line).start()

    lane = lax.broadcasted_iota(jnp.int32, (8, 128), 1)
    id_bf16 = ids.astype(F32).astype(BF16)

    def weigh(sel, logits, expert):
        named = dot_nt(sel.astype(BF16), id_bf16)
        near = jnp.zeros((8, 128), F32)
        every = jnp.zeros((8, 128), F32)
        for s in range(chips):
            number = (lane // router_rows) * (chips * router_rows) + s * router_rows + lane % router_rows
            number = jnp.where(lane < 2 * router_rows, number, -1)
            score = 1.0 / (1.0 + jnp.exp(-logits[s]))
            near += jnp.where(number == expert, score, 0.0)
            match = number.astype(F32) == named[:, 0:1]
            for k in range(1, ids.shape[0]):
                match |= number.astype(F32) == named[:, k : k + 1]
            every += jnp.where(match, score, 0.0)
        near = jnp.sum(near, axis=1, keepdims=True)
        every = jnp.sum(every, axis=1, keepdims=True)
        return route_scale * near / every

    def split(total, weight):
        j = lax.broadcasted_iota(jnp.int32, (8, 1), 0)
        both = []
        for side in range(2):
            v = jnp.where(j // 4 == pool, total[side * 8 : side * 8 + 8] * weight, 0.0)
            hi = v.astype(BF16).astype(F32)
            both.append(jnp.concatenate([hi, v - hi], axis=0).astype(BF16))
        return both

    for step in range(1, chips):
        c = lax.rem(dev + step, chips)
        pltpu.make_async_copy(logit_in.at[c], logit_in.at[c], log_recv.at[c]).wait()
    peer_logits = to_peer(logit_in, logit_peer, 2 * PIECES + 1)
    peer_logits.start()
    own_weight = weigh(sel_own, logit_in, pool)

    def paired(p, z):
        x_copy(p, z).wait_recv()
        return parts[p, z * PAIR + pair].astype(F32) + from_x[p, z].astype(F32)

    def go_up(p, z):
        total = paired(p, z)

        @pl.when(line > 0)
        def _():
            up_copy(p, z).wait_recv()
            sums[p, z] = (total + from_up[p, z].astype(F32)).astype(BF16)

        @pl.when(line == 0)
        def _():
            sums[p, z] = total.astype(BF16)

        up_copy(p, z).start()

    def go_down(p, z):
        total = paired(p, z)

        @pl.when(line < LINE - 1)
        def _():
            down_copy(p, z).wait_recv()
            sums[p, z] = (total + from_down[p, z].astype(F32)).astype(BF16)

        @pl.when(line == LINE - 1)
        def _():
            sums[p, z] = total.astype(BF16)

        down_copy(p, z).start()

    peer_total = [
        to_peer(total_v.at[p], total_peer.at[p], PIECES + p) for p in range(PIECES)
    ]

    def finish(p):
        total_v[p] = paired(p, line)

        @pl.when(line > 0)
        def _():
            up_copy(p, line).wait_recv()
            total_v[p] += from_up[p, line].astype(F32)

        @pl.when(line < LINE - 1)
        def _():
            down_copy(p, line).wait_recv()
            total_v[p] += from_down[p, line].astype(F32)

        peer_total[p].start()

    for p in range(PIECES):
        each_far_first(lambda z: go_up(p, z), lambda z: go_down(p, z))
        if p:
            finish(p - 1)
    peer_logits.wait_recv()
    other_weight = weigh(sel_other, logit_peer, 1 - pool)

    def mix(sel, weight):
        return jnp.where(sel > 0.5, jnp.broadcast_to(weight * 0.0 + 1.0, sel.shape), 0.0)

    own_mix, other_mix = mix(sel_own, own_weight), mix(sel_other, other_weight)
    mixing = jnp.concatenate([own_mix, own_mix, other_mix, other_mix], axis=0).astype(BF16)
    own_weight = jnp.where(own_weight == own_weight, own_weight, 0.0)
    other_weight = jnp.where(other_weight == other_weight, other_weight, 0.0)
    finish(PIECES - 1)

    def give(p, total, weight, first):
        left, right = split(total, weight)
        values[first : first + 16, p * piece : (p + 1) * piece] = left
        values[first : first + 16, half + p * piece : half + (p + 1) * piece] = right

    for p in range(PIECES):
        give(p, total_v[p], own_weight, 0)
    for p in range(PIECES):
        peer_total[p].wait_recv()
        give(p, total_peer[p], other_weight, 16)
        for low in (p * piece, half + p * piece):
            out[:, low : low + piece] = dot_tn(mixing, values[:, low : low + piece]).astype(BF16)

    for copy in (*peer_rows, peer_router, peer_logits, *peer_total):
        copy.wait_send()
    for p, z in [(p, z) for p in range(PIECES) for z in range(LINE)]:
        row_copy(p, z, across, row_x).wait_send()
        x_copy(p, z).wait_send()

        @pl.when((line < LINE - 1) & (z <= line))
        def _():
            row_copy(p, z, dev + PAIR, row_up).wait_send()

        @pl.when((line > 0) & (z >= line))
        def _():
            row_copy(p, z, dev - PAIR, row_down).wait_send()

        @pl.when(z > line)
        def _():
            up_copy(p, z).wait_send()

        @pl.when(z < line)
        def _():
            down_copy(p, z).wait_send()

    for step in range(1, chips):
        log_copy(step).wait_send()


def fused(tokens, routes, router, w_gate, w_up, w_down):
    batches, block, width = tokens.shape
    half = width // 2
    chips = LINE * PAIR
    n_rows = batches * block
    vmem = pl.BlockSpec(memory_space=pltpu.VMEM)
    hbm = pl.BlockSpec(memory_space=pltpu.HBM)
    dma = pltpu.SemaphoreType.DMA
    out = pl.pallas_call(
        kernel,
        out_shape=jax.ShapeDtypeStruct((n_rows, width), BF16),
        in_specs=[hbm, vmem, hbm, hbm, hbm, hbm],
        out_specs=vmem,
        scratch_shapes=[
            pltpu.VMEM((n_rows, width), BF16),
            pltpu.VMEM((32, width), BF16),
            pltpu.VMEM(w_gate.shape, BF16),
            pltpu.VMEM(w_up.shape, BF16),
            pltpu.VMEM(w_down.shape, BF16),
            pltpu.VMEM((2, router.shape[0], width), BF16),
            pltpu.VMEM((PIECES, 16, half // PIECES), BF16),
            pltpu.VMEM((PIECES, 16, half // PIECES), BF16),
            pltpu.VMEM((PIECES, chips, 16, half // PIECES), BF16),
            pltpu.VMEM((PIECES, chips, 16, half // PIECES), BF16),
            pltpu.VMEM((PIECES, LINE, 16, half // PIECES), BF16),
            pltpu.VMEM((PIECES, LINE, 16, half // PIECES), BF16),
            pltpu.VMEM((PIECES, LINE, 16, half // PIECES), BF16),
            pltpu.VMEM((PIECES, LINE, 16, half // PIECES), BF16),
            pltpu.VMEM((PIECES, 16, half // PIECES), F32),
            pltpu.VMEM((PIECES, 16, half // PIECES), F32),
            pltpu.VMEM((chips, 8, 128), F32),
            pltpu.VMEM((chips, 8, 128), F32),
            pltpu.VMEM((chips, 8, 128), F32),
            dma((5,)), dma((2 * PIECES + 2,)), dma((2 * PIECES + 2,)), dma((PIECES, chips)),
            dma((PIECES, LINE)), dma((PIECES, LINE)), dma((PIECES, LINE)),
            dma((chips,)), dma((chips,)), dma((PIECES, LINE)), dma((PIECES, LINE)),
            dma((PIECES, LINE)), dma((PIECES, LINE)), dma((PIECES, LINE)), dma((PIECES, LINE)),
        ],
        compiler_params=pltpu.CompilerParams(
            collective_id=0, has_side_effects=True, vmem_limit_bytes=(64 << 20) - (12288 << 10)
        ),
    )(tokens.reshape(n_rows, width), routes.transpose(0, 2, 1), router, w_gate, w_up, w_down)
    return out.reshape(tokens.shape)


def spread(tokens, routes, router, w_gate, w_up, w_down):
    groups = lax.axis_size(("pool", "dev"))
    batches = tokens.shape[0]
    model_width = tokens.shape[2]
    hidden_width = w_gate.shape[1]
    slices = FF // hidden_width
    experts_win = groups // slices
    capacity = CAP
    logits = jnp.einsum(
        "mrd,ed->mre",
        tokens,
        lax.all_gather(router, ("pool", "dev"), axis=0, tiled=True),
        preferred_element_type=jnp.float32,
    )
    scores = jax.nn.sigmoid(logits)
    expert_ids = jnp.arange(logits.shape[2], dtype=jnp.int32)
    picked = routes[..., None] == expert_ids
    chosen = jnp.sum(jnp.where(picked, scores[:, :, None, :], 0.0), axis=-1)
    weights = route_scale * chosen / jnp.sum(chosen, axis=-1, keepdims=True)
    window = picked[..., :experts_win]
    route_weight = jnp.sum(jnp.where(window, weights[..., None], 0.0), axis=2)
    routed = jnp.any(window, axis=2).astype(jnp.int32)
    position = jnp.cumsum(routed, axis=1) - 1
    slot_ids = jnp.arange(capacity, dtype=jnp.int32)
    selector = (routed[..., None] == 1) & (position[..., None] == slot_ids)
    slot_rows = jnp.einsum(
        "mrec,mrd->mecd", selector.astype(jnp.bfloat16), tokens, preferred_element_type=jnp.float32
    ).astype(jnp.bfloat16)
    outgoing = jnp.broadcast_to(
        slot_rows[:, :, None], (batches, experts_win, slices, capacity, model_width)
    )
    outgoing = outgoing.reshape(batches, groups, capacity, model_width)
    arrived = lax.all_to_all(outgoing, ("pool", "dev"), split_axis=1, concat_axis=1, tiled=True)
    flat_rows = arrived.reshape(-1, model_width)
    gate_proj = jnp.dot(flat_rows, w_gate, preferred_element_type=jnp.float32)
    up_proj = jnp.dot(flat_rows, w_up, preferred_element_type=jnp.float32)
    hidden = (jax.nn.silu(gate_proj) * up_proj).astype(jnp.bfloat16)
    partial_value = jnp.dot(hidden, w_down, preferred_element_type=jnp.float32).astype(jnp.bfloat16)
    send_partial_value = partial_value.reshape(arrived.shape)
    returned = lax.all_to_all(
        send_partial_value, ("pool", "dev"), split_axis=1, concat_axis=1, tiled=True
    )
    returned = returned.reshape(batches, experts_win, slices, capacity, model_width)
    expert_out = jnp.sum(returned, axis=2, dtype=jnp.float32)
    mixing = selector.astype(jnp.float32) * route_weight[..., None]
    combined = jnp.einsum("mrec,mecd->mrd", mixing, expert_out, precision=lax.Precision.HIGHEST)
    return combined.astype(jnp.bfloat16)


def solution(mesh):
    shape = dict(mesh.shape)
    per_device = fused if (shape["pool"], shape["dev"]) == (2, LINE * PAIR) else spread
    placed = (
        P(None, ("group", "pool", "dev"), None),
        P(None, ("group", "pool", "dev"), None),
        P(("pool", "dev"), None),
        P(None, ("pool", "dev")),
        P(None, ("pool", "dev")),
        P(("pool", "dev"), None),
    )
    return jax.shard_map(
        per_device,
        mesh=mesh,
        in_specs=placed,
        out_specs=P(None, ("group", "pool", "dev"), None),
        check_vma=False,
    )
```

```python
import functools

import jax
import jax.numpy as jnp
from jax import lax
from jax.experimental import pallas as pl
from jax.experimental.pallas import tpu as pltpu
from jax.sharding import PartitionSpec as P

FF = 2048
CAP = 2
LINE = 4
PAIR = 2
PIECES = 2

route_scale = 2.5
MESH = pl.DeviceIdType.MESH
F32 = jnp.float32
BF16 = jnp.bfloat16


def dot(a, b):
    return jnp.dot(a, b, preferred_element_type=F32)


def dot_tn(a, b):
    return lax.dot_general(a, b, (((0,), (0,)), ((), ())), preferred_element_type=F32)


def dot_nt(a, b):
    return lax.dot_general(a, b, (((1,), (1,)), ((), ())), preferred_element_type=F32)


def kernel(
    tokens, routes, router, w_gate, w_up, w_down, out,
    values, gate_v, up_v, down_v, router_v, mine, theirs, rows, parts, from_x, from_up, from_down, sums,
    total_v, total_peer, logit_out, logit_in, logit_peer,
    load_sem, peer_send, peer_recv, row_recv, row_up, row_down, row_x,
    log_send, log_recv, x_send, x_recv, up_send, up_recv, down_send, down_recv,
):
    pool, dev = lax.axis_index("pool"), lax.axis_index("dev")
    chips = LINE * PAIR
    line, pair = dev // PAIR, dev % PAIR
    n_rows, width = tokens.shape
    half = width // 2
    piece = half // PIECES
    block = n_rows // 2
    router_rows = router.shape[0]

    own_router = pltpu.make_async_copy(router, router_v.at[pool], load_sem.at[3])
    own_router.start()
    loads = [
        pltpu.make_async_copy(w_gate, gate_v, load_sem.at[0]),
        pltpu.make_async_copy(w_up, up_v, load_sem.at[1]),
        pltpu.make_async_copy(w_down, down_v, load_sem.at[2]),
    ]
    barrier = pltpu.get_barrier_semaphore()
    pl.semaphore_signal(barrier, inc=1, device_id={"pool": 1 - pool}, device_id_type=MESH)
    for step in range(1, chips):
        pl.semaphore_signal(
            barrier, inc=1, device_id={"dev": lax.rem(dev + step, chips)}, device_id_type=MESH
        )

    ids = jnp.concatenate([routes[0], routes[1]], axis=1)
    slot_no = lax.broadcasted_iota(jnp.int32, (8, n_rows), 0)
    row_no = lax.broadcasted_iota(jnp.int32, (8, n_rows), 1)
    place = (row_no // block == (slot_no % 4) // 2) & (slot_no // 4 == pool)
    r0 = lax.broadcasted_iota(jnp.int32, (n_rows, n_rows), 0)
    r1 = lax.broadcasted_iota(jnp.int32, (n_rows, n_rows), 1)
    earlier = ((r0 < r1) & (r0 // block == r1 // block)).astype(F32).astype(BF16)

    def select(expert):
        named = jnp.max((ids == expert).astype(F32), axis=0, keepdims=True)
        named = jnp.broadcast_to(named, (8, n_rows))
        count = dot(named.astype(BF16), earlier)
        hit = (named > 0.5) & place & (count == (slot_no % 2).astype(F32))
        return hit.astype(F32)

    def in_slots(sel, p):
        sel = sel.astype(BF16)
        left = dot(sel, tokens[:, p * piece : (p + 1) * piece])
        right = dot(sel, tokens[:, half + p * piece : half + (p + 1) * piece])
        return jnp.concatenate([left, right], axis=0).astype(BF16)

    sel_own, sel_other = select(pool), select(1 - pool)
    for p in range(PIECES):
        mine[p] = in_slots(sel_other, p)

    pl.semaphore_wait(barrier, chips)

    def to_peer(src, dst, k):
        return pltpu.make_async_remote_copy(
            src, dst, peer_send.at[k], peer_recv.at[k],
            device_id={"pool": 1 - pool}, device_id_type=MESH,
        )

    peer_rows = [to_peer(mine.at[p], theirs.at[p], p) for p in range(PIECES)]
    for copy in peer_rows:
        copy.start()
    peer_router = to_peer(router, router_v.at[pool], 2 * PIECES)
    peer_router.start()

    def row_copy(p, z, target, sems):
        c = z * PAIR + pair
        return pltpu.make_async_remote_copy(
            rows.at[p, c], rows.at[p, c], sems.at[p, z], row_recv.at[p, c],
            device_id={"dev": target}, device_id_type=MESH,
        )

    def row_wait(p, c):
        pltpu.make_async_copy(rows.at[p, c], rows.at[p, c], row_recv.at[p, c]).wait()

    across = line * PAIR + 1 - pair
    for p in range(PIECES):
        own = in_slots(sel_own, p)
        peer_rows[p].wait_recv()
        rows[p, dev] = own + theirs[p]

        @pl.when(line < LINE - 1)
        def _():
            row_copy(p, line, dev + PAIR, row_up).start()

        @pl.when(line > 0)
        def _():
            row_copy(p, line, dev - PAIR, row_down).start()

        row_copy(p, line, across, row_x).start()

    for load in loads:
        load.start()
    for d in range(1, LINE):
        for p in range(PIECES):
            @pl.when(line - d >= 0)
            def _():
                z = line - d
                row_wait(p, z * PAIR + pair)

                @pl.when(line < LINE - 1)
                def _():
                    row_copy(p, z, dev + PAIR, row_up).start()

                row_copy(p, z, across, row_x).start()

            @pl.when(line + d < LINE)
            def _():
                z = line + d
                row_wait(p, z * PAIR + pair)

                @pl.when(line > 0)
                def _():
                    row_copy(p, z, dev - PAIR, row_down).start()

                row_copy(p, z, across, row_x).start()

    own_router.wait()
    peer_router.wait_recv()
    for load in loads:
        load.wait()
    for p in range(PIECES):
        for z in range(LINE):
            row_wait(p, z * PAIR + 1 - pair)

    hid = gate_v.shape[1]

    def project(side):
        def body(k, carry):
            g, u, l = carry
            deep = pl.multiple_of(side * half + k * piece, 128)
            a = rows[k].reshape(chips * 16, piece)
            r = router_v[:, :, pl.ds(deep, piece)].reshape(2 * router_rows, piece)
            g = g + dot(a, gate_v[pl.ds(deep, piece), :])
            u = u + dot(a, up_v[pl.ds(deep, piece), :])
            l = l + dot_nt(a, r)
            return g, u, l

        zero = jnp.zeros((chips * 16, hid), F32)
        got = lax.fori_loop(
            0, PIECES, body, (zero, zero, jnp.zeros((chips * 16, 2 * router_rows), F32))
        )
        return [v.reshape(chips, 16, v.shape[1])[:, side * 8 : side * 8 + 8] for v in got]

    (gl, ul, ll), (gr, ur, lr) = project(0), project(1)
    gate, up = gl + gr, ul + ur
    hidden = (gate / (1.0 + jnp.exp(-gate)) * up).astype(F32).reshape(chips * 8, hid).astype(BF16)
    logit_out[:, :, 0 : 2 * router_rows] = ll + lr
    logit_out[:, :, 2 * router_rows :] = jnp.zeros((chips, 8, 128 - 2 * router_rows), F32)
    logit_in[dev] = logit_out[dev]

    def log_copy(step):
        to = lax.rem(dev + step, chips)
        return pltpu.make_async_remote_copy(
            logit_out.at[to], logit_in.at[dev], log_send.at[step], log_recv.at[dev],
            device_id={"dev": to}, device_id_type=MESH,
        )

    for step in range(1, chips):
        log_copy(step).start()

    def x_copy(p, z):
        return pltpu.make_async_remote_copy(
            parts.at[p, z * PAIR + 1 - pair], from_x.at[p, z], x_send.at[p, z], x_recv.at[p, z],
            device_id={"dev": across}, device_id_type=MESH,
        )

    def up_copy(p, z):
        return pltpu.make_async_remote_copy(
            sums.at[p, z], from_up.at[p, z], up_send.at[p, z], up_recv.at[p, z],
            device_id={"dev": dev + PAIR}, device_id_type=MESH,
        )

    def down_copy(p, z):
        return pltpu.make_async_remote_copy(
            sums.at[p, z], from_down.at[p, z], down_send.at[p, z], down_recv.at[p, z],
            device_id={"dev": dev - PAIR}, device_id_type=MESH,
        )

    def each_far_first(act_up, act_down):
        for d in range(LINE - 1, 0, -1):
            @pl.when(line + d < LINE)
            def _():
                act_up(line + d)

            @pl.when(line - d >= 0)
            def _():
                act_down(line - d)

    for p in range(PIECES):
        left = dot(hidden, down_v[:, p * piece : (p + 1) * piece])
        right = dot(hidden, down_v[:, half + p * piece : half + (p + 1) * piece])
        both = [left.reshape(chips, 8, piece), right.reshape(chips, 8, piece)]
        parts[p] = jnp.concatenate(both, axis=1).astype(BF16)
        each_far_first(lambda z: x_copy(p, z).start(), lambda z: x_copy(p, z).start())
        x_copy(p, line).start()

    lane = lax.broadcasted_iota(jnp.int32, (8, 128), 1)
    id_bf16 = ids.astype(F32).astype(BF16)

    def weigh(sel, logits, expert):
        named = dot_nt(sel.astype(BF16), id_bf16)
        near = jnp.zeros((8, 128), F32)
        every = jnp.zeros((8, 128), F32)
        for s in range(chips):
            number = (lane // router_rows) * (chips * router_rows) + s * router_rows + lane % router_rows
            number = jnp.where(lane < 2 * router_rows, number, -1)
            score = 1.0 / (1.0 + jnp.exp(-logits[s]))
            near += jnp.where(number == expert, score, 0.0)
            match = number.astype(F32) == named[:, 0:1]
            for k in range(1, ids.shape[0]):
                match |= number.astype(F32) == named[:, k : k + 1]
            every += jnp.where(match, score, 0.0)
        near = jnp.sum(near, axis=1, keepdims=True)
        every = jnp.sum(every, axis=1, keepdims=True)
        return route_scale * near / every

    def split(total, weight):
        j = lax.broadcasted_iota(jnp.int32, (8, 1), 0)
        both = []
        for side in range(2):
            v = jnp.where(j // 4 == pool, total[side * 8 : side * 8 + 8] * weight, 0.0)
            hi = v.astype(BF16).astype(F32)
            both.append(jnp.concatenate([hi, v - hi], axis=0).astype(BF16))
        return both

    for step in range(1, chips):
        c = lax.rem(dev + step, chips)
        pltpu.make_async_copy(logit_in.at[c], logit_in.at[c], log_recv.at[c]).wait()
    peer_logits = to_peer(logit_in, logit_peer, 2 * PIECES + 1)
    peer_logits.start()
    own_weight = weigh(sel_own, logit_in, pool)

    def paired(p, z):
        x_copy(p, z).wait_recv()
        return parts[p, z * PAIR + pair].astype(F32) + from_x[p, z].astype(F32)

    def go_up(p, z):
        total = paired(p, z)

        @pl.when(line > 0)
        def _():
            up_copy(p, z).wait_recv()
            sums[p, z] = (total + from_up[p, z].astype(F32)).astype(BF16)

        @pl.when(line == 0)
        def _():
            sums[p, z] = total.astype(BF16)

        up_copy(p, z).start()

    def go_down(p, z):
        total = paired(p, z)

        @pl.when(line < LINE - 1)
        def _():
            down_copy(p, z).wait_recv()
            sums[p, z] = (total + from_down[p, z].astype(F32)).astype(BF16)

        @pl.when(line == LINE - 1)
        def _():
            sums[p, z] = total.astype(BF16)

        down_copy(p, z).start()

    peer_total = [
        to_peer(total_v.at[p], total_peer.at[p], PIECES + p) for p in range(PIECES)
    ]

    def finish(p):
        total_v[p] = paired(p, line)

        @pl.when(line > 0)
        def _():
            up_copy(p, line).wait_recv()
            total_v[p] += from_up[p, line].astype(F32)

        @pl.when(line < LINE - 1)
        def _():
            down_copy(p, line).wait_recv()
            total_v[p] += from_down[p, line].astype(F32)

        peer_total[p].start()

    for p in range(PIECES):
        each_far_first(lambda z: go_up(p, z), lambda z: go_down(p, z))
        if p:
            finish(p - 1)
    peer_logits.wait_recv()
    other_weight = weigh(sel_other, logit_peer, 1 - pool)

    def mix(sel, weight):
        return jnp.where(sel > 0.5, jnp.broadcast_to(weight * 0.0 + 1.0, sel.shape), 0.0)

    own_mix, other_mix = mix(sel_own, own_weight), mix(sel_other, other_weight)
    mixing = jnp.concatenate([own_mix, own_mix, other_mix, other_mix], axis=0).astype(BF16)
    own_weight = jnp.where(own_weight == own_weight, own_weight, 0.0)
    other_weight = jnp.where(other_weight == other_weight, other_weight, 0.0)
    finish(PIECES - 1)

    def give(p, total, weight, first):
        left, right = split(total, weight)
        values[first : first + 16, p * piece : (p + 1) * piece] = left
        values[first : first + 16, half + p * piece : half + (p + 1) * piece] = right

    for p in range(PIECES):
        give(p, total_v[p], own_weight, 0)
    for p in range(PIECES):
        peer_total[p].wait_recv()
        give(p, total_peer[p], other_weight, 16)
        for low in (p * piece, half + p * piece):
            out[:, low : low + piece] = dot_tn(mixing, values[:, low : low + piece]).astype(BF16)

    for copy in (*peer_rows, peer_router, peer_logits, *peer_total):
        copy.wait_send()
    for p, z in [(p, z) for p in range(PIECES) for z in range(LINE)]:
        row_copy(p, z, across, row_x).wait_send()
        x_copy(p, z).wait_send()

        @pl.when((line < LINE - 1) & (z <= line))
        def _():
            row_copy(p, z, dev + PAIR, row_up).wait_send()

        @pl.when((line > 0) & (z >= line))
        def _():
            row_copy(p, z, dev - PAIR, row_down).wait_send()

        @pl.when(z > line)
        def _():
            up_copy(p, z).wait_send()

        @pl.when(z < line)
        def _():
            down_copy(p, z).wait_send()

    for step in range(1, chips):
        log_copy(step).wait_send()


def fused(tokens, routes, router, w_gate, w_up, w_down):
    batches, block, width = tokens.shape
    half = width // 2
    chips = LINE * PAIR
    n_rows = batches * block
    vmem = pl.BlockSpec(memory_space=pltpu.VMEM)
    hbm = pl.BlockSpec(memory_space=pltpu.HBM)
    dma = pltpu.SemaphoreType.DMA
    out = pl.pallas_call(
        kernel,
        out_shape=jax.ShapeDtypeStruct((n_rows, width), BF16),
        in_specs=[vmem, vmem, vmem, hbm, hbm, hbm],
        out_specs=vmem,
        scratch_shapes=[
            pltpu.VMEM((32, width), BF16),
            pltpu.VMEM(w_gate.shape, BF16),
            pltpu.VMEM(w_up.shape, BF16),
            pltpu.VMEM(w_down.shape, BF16),
            pltpu.VMEM((2, router.shape[0], width), BF16),
            pltpu.VMEM((PIECES, 16, half // PIECES), BF16),
            pltpu.VMEM((PIECES, 16, half // PIECES), BF16),
            pltpu.VMEM((PIECES, chips, 16, half // PIECES), BF16),
            pltpu.VMEM((PIECES, chips, 16, half // PIECES), BF16),
            pltpu.VMEM((PIECES, LINE, 16, half // PIECES), BF16),
            pltpu.VMEM((PIECES, LINE, 16, half // PIECES), BF16),
            pltpu.VMEM((PIECES, LINE, 16, half // PIECES), BF16),
            pltpu.VMEM((PIECES, LINE, 16, half // PIECES), BF16),
            pltpu.VMEM((PIECES, 16, half // PIECES), F32),
            pltpu.VMEM((PIECES, 16, half // PIECES), F32),
            pltpu.VMEM((chips, 8, 128), F32),
            pltpu.VMEM((chips, 8, 128), F32),
            pltpu.VMEM((chips, 8, 128), F32),
            dma((4,)), dma((2 * PIECES + 2,)), dma((2 * PIECES + 2,)), dma((PIECES, chips)),
            dma((PIECES, LINE)), dma((PIECES, LINE)), dma((PIECES, LINE)),
            dma((chips,)), dma((chips,)), dma((PIECES, LINE)), dma((PIECES, LINE)),
            dma((PIECES, LINE)), dma((PIECES, LINE)), dma((PIECES, LINE)), dma((PIECES, LINE)),
        ],
        compiler_params=pltpu.CompilerParams(
            collective_id=0, has_side_effects=True, vmem_limit_bytes=(64 << 20) - (12288 << 10)
        ),
    )(tokens.reshape(n_rows, width), routes.transpose(0, 2, 1), router, w_gate, w_up, w_down)
    return out.reshape(tokens.shape)


def spread(tokens, routes, router, w_gate, w_up, w_down):
    groups = lax.axis_size(("pool", "dev"))
    batches = tokens.shape[0]
    model_width = tokens.shape[2]
    hidden_width = w_gate.shape[1]
    slices = FF // hidden_width
    experts_win = groups // slices
    capacity = CAP
    logits = jnp.einsum(
        "mrd,ed->mre",
        tokens,
        lax.all_gather(router, ("pool", "dev"), axis=0, tiled=True),
        preferred_element_type=jnp.float32,
    )
    scores = jax.nn.sigmoid(logits)
    expert_ids = jnp.arange(logits.shape[2], dtype=jnp.int32)
    picked = routes[..., None] == expert_ids
    chosen = jnp.sum(jnp.where(picked, scores[:, :, None, :], 0.0), axis=-1)
    weights = route_scale * chosen / jnp.sum(chosen, axis=-1, keepdims=True)
    window = picked[..., :experts_win]
    route_weight = jnp.sum(jnp.where(window, weights[..., None], 0.0), axis=2)
    routed = jnp.any(window, axis=2).astype(jnp.int32)
    position = jnp.cumsum(routed, axis=1) - 1
    slot_ids = jnp.arange(capacity, dtype=jnp.int32)
    selector = (routed[..., None] == 1) & (position[..., None] == slot_ids)
    slot_rows = jnp.einsum(
        "mrec,mrd->mecd", selector.astype(jnp.bfloat16), tokens, preferred_element_type=jnp.float32
    ).astype(jnp.bfloat16)
    outgoing = jnp.broadcast_to(
        slot_rows[:, :, None], (batches, experts_win, slices, capacity, model_width)
    )
    outgoing = outgoing.reshape(batches, groups, capacity, model_width)
    arrived = lax.all_to_all(outgoing, ("pool", "dev"), split_axis=1, concat_axis=1, tiled=True)
    flat_rows = arrived.reshape(-1, model_width)
    gate_proj = jnp.dot(flat_rows, w_gate, preferred_element_type=jnp.float32)
    up_proj = jnp.dot(flat_rows, w_up, preferred_element_type=jnp.float32)
    hidden = (jax.nn.silu(gate_proj) * up_proj).astype(jnp.bfloat16)
    partial_value = jnp.dot(hidden, w_down, preferred_element_type=jnp.float32).astype(jnp.bfloat16)
    send_partial_value = partial_value.reshape(arrived.shape)
    returned = lax.all_to_all(
        send_partial_value, ("pool", "dev"), split_axis=1, concat_axis=1, tiled=True
    )
    returned = returned.reshape(batches, experts_win, slices, capacity, model_width)
    expert_out = jnp.sum(returned, axis=2, dtype=jnp.float32)
    mixing = selector.astype(jnp.float32) * route_weight[..., None]
    combined = jnp.einsum("mrec,mecd->mrd", mixing, expert_out, precision=lax.Precision.HIGHEST)
    return combined.astype(jnp.bfloat16)


def solution(mesh):
    shape = dict(mesh.shape)
    per_device = fused if (shape["pool"], shape["dev"]) == (2, LINE * PAIR) else spread
    placed = (
        P(None, ("group", "pool", "dev"), None),
        P(None, ("group", "pool", "dev"), None),
        P(("pool", "dev"), None),
        P(None, ("pool", "dev")),
        P(None, ("pool", "dev")),
        P(("pool", "dev"), None),
    )
    return jax.shard_map(
        per_device,
        mesh=mesh,
        in_specs=placed,
        out_specs=P(None, ("group", "pool", "dev"), None),
        check_vma=False,
    )
```
